256 devices in a mesh: pipe: 8 (over z_lo, core), expert: 32 (over y, z_hi, x).
Axes of the slice: x: 4, y: 4, z: 8 (z_hi: 2, z_lo: 4; z = z_hi * 4 + z_lo), core: 2. Of those that a mesh axis runs over, the one named last changes fastest.
Arguments:
- tokens: bfloat16 [32768, 7168], P(('pipe', 'expert')), may hold values from -6 to 6
- cotangent: bfloat16 [32768, 7168], P(('pipe', 'expert')), may hold values from -6 to 6
- expert_ids: int32 [32768, 8], P(('pipe', 'expert')), may hold values from 0 to 255, all different within a row; in each aligned block of 128 rows (0 to 127, 128 to 255, ...) at most 8 rows name the same one
- gate_weights: float32 [32768, 8], P(('pipe', 'expert')), may hold values from 0.1 to 0.6
- w_gate: bfloat16 [8, 3584, 4096], P('pipe', None, 'expert'), may hold values from -0.0625 to 0.0625
- w_up: bfloat16 [8, 3584, 4096], P('pipe', None, 'expert'), may hold values from -0.0625 to 0.0625
- w_down: bfloat16 [8, 4096, 3584], P('pipe', 'expert'), may hold values from -0.1875 to 0.1875
Outputs:
- mixed_out: bfloat16 [32768, 7168], P(('pipe', 'expert'))
- input_grad: bfloat16 [32768, 7168], P(('pipe', 'expert'))
- grad_gate: bfloat16 [8, 3584, 4096], P('pipe', None, 'expert')
- grad_up: bfloat16 [8, 3584, 4096], P('pipe', None, 'expert')
- grad_down: bfloat16 [8, 4096, 3584], P('pipe', 'expert')
The draws below stay inside these ranges and needn't reach their ends.
Inputs may be any that keep to these rules, and one draw needn't show every extreme that they name: `expert_ids`: the 8 entries of a row differ. In each block of 128 rows, no expert is named more than 8 times, a bound that some block reaches.
All inputs are finite; a program needn't handle non-finite values.
Results may differ from the reference program's by a relative error of at most 0.0065.
Values may be sent and summed in bfloat16 or wider, within the bound.
A program may use at most 128 MiB of HBM per device.

```python
import math
import jax
import jax.numpy as jnp
import numpy as np
from jax import lax

D = 7168
HE = 1024
ROUTED = 256
TOP = 8
GROUP = 8
TOK_DEV = 128
CAP = 8
HE_DEV = 128
D2 = 3584
EXPERTS = 4
TOKENS = 32768
N_PIPE = 8
N_EXPERT = 32


def level_of(own_key, dims, split, smallest, high):
    loudness, own = 1.0, jax.random.fold_in(own_key, 6)
    for position, parts in split:
        draws = jnp.exp(jax.random.uniform(jax.random.fold_in(own, position), (parts,), jnp.float32, smallest / len(split), high / len(split)))
        loudness = loudness * jnp.repeat(draws, dims[position] // parts).reshape([-1 if axis == position else 1 for axis in range(len(dims))])
    return loudness


def assign_block(own_key, own, number, rows, count, top, most, slope):
    sequence = jax.random.permutation(own_key, count)
    heavy_load, ordinary = load_shares(count, rows * top, most, slope, True), load_shares(count, rows * top, most, slope, False)
    places = jnp.arange(count)

    def named(tallies, turn):
        used = int((tallies > 0).sum())
        fixed = max(1, used // 4)
        moved = fixed + (places - fixed + turn * (used - fixed)) % max(1, count - fixed)
        return jnp.zeros((count,), jnp.int32).at[sequence[jnp.where(places < fixed, places, moved)]].set(jnp.asarray(tallies, jnp.int32))

    tallies = jnp.where(number % 4 == 0, named(heavy_load, number // 4), named(ordinary, number - number // 4 - 1))
    mixed = jax.random.permutation(jax.random.fold_in(own, 3), count)
    source_of, sink = mixed[0:count // 2 * 2:2], mixed[1:count // 2 * 2:2]
    room = jnp.minimum(tallies[source_of] - 1, most - tallies[sink]) // 2
    room = jnp.where((source_of == sequence[0]) | (sink == sequence[0]) | (tallies[sink] == 0), 0, jnp.maximum(room, 0))
    moved = jax.random.randint(jax.random.fold_in(own, 4), (count // 2,), 0, 1 << 20) % (room + 1)
    tallies = tallies.at[source_of].add(-moved).at[sink].add(moved)
    items = jnp.searchsorted(jnp.cumsum(tallies), jnp.arange(rows * top), side="right").astype(jnp.int32)
    grid = items.reshape(top, rows).T
    grid = grid[jax.random.permutation(jax.random.fold_in(own, 1), rows)]
    turn = jax.random.randint(jax.random.fold_in(own, 2), (rows, 1), 0, top)
    return jnp.take_along_axis(grid, (jnp.arange(top)[None, :] + turn) % top, axis=1)


def load_shares(number_of, total, limit, slope, full):
    loads = [(1 << 20) // math.isqrt(rank ** slope) + 1 for rank in range(1, number_of + 1)]
    largest = limit if full else min(limit, max(-(-total // number_of), total * loads[0] // sum(loads)))
    least = 1 if total - largest >= number_of - 1 else 0
    counts, surplus = [largest] + [least] * (number_of - 1), total - largest - least * (number_of - 1)
    while surplus > 0:
        free = [i for i in range(1, number_of) if counts[i] < largest] or [i for i in range(1, number_of) if counts[i] < limit]
        whole, left = sum([loads[i] for i in free]), surplus
        for i in free:
            addition = min(limit - counts[i], max(1, left * loads[i] // whole), surplus)
            counts[i] = counts[i] + addition
            surplus = surplus - addition
    return np.array(counts)


def gaussian(stream_key, shape, spread, reach, cuts=(), kind=jnp.bfloat16):
    values = jax.random.normal(stream_key, shape, jnp.float32) * spread
    if len(cuts) > 0:
        values = level_of(stream_key, shape, cuts, -0.22, 0.18) * values
    return jnp.clip(values, min=-reach, max=reach).astype(kind)


def setup_inputs(seed: int = 0) -> dict:
    splits = jax.random.split(jax.random.key(seed), 8)
    tokens = gaussian(splits[0], (TOKENS, D), 1.0, 6.0, ((0, 256),))
    cotangent = gaussian(splits[1], (TOKENS, D), 1.0, 6.0, ((0, 256),))
    expert_ids_keys = jax.random.split(jax.random.fold_in(splits[2], 1), TOKENS // TOK_DEV)
    expert_ids_turns = jax.random.permutation(jax.random.fold_in(splits[2], 3), TOKENS // TOK_DEV)
    expert_ids = jax.vmap(lambda own, number: assign_block(jax.random.fold_in(splits[2], 2), own, number, TOK_DEV, ROUTED, TOP, CAP, 2))(expert_ids_keys, expert_ids_turns).reshape((TOKENS, TOP))
    gate_weights = jnp.clip(0.1 + 0.5 * jax.random.uniform(splits[3], (TOKENS, TOP), jnp.float32) ** level_of(splits[3], (TOKENS, TOP), ((0, 256),), -0.2, 0.2), 0.1, 0.6)
    w_gate = gaussian(splits[4], (N_PIPE, D2, EXPERTS * HE), D ** -0.5, 0.0625, ((0, 8), (2, 32)))
    w_up = gaussian(splits[5], (N_PIPE, D2, EXPERTS * HE), D ** -0.5, 0.0625, ((0, 8), (2, 32)))
    w_down = gaussian(splits[6], (N_PIPE, EXPERTS * HE, D2), HE ** -0.5, 0.1875, ((0, 8), (1, 32)))
    return {"tokens": tokens, "cotangent": cotangent, "expert_ids": expert_ids, "gate_weights": gate_weights, "w_gate": w_gate, "w_up": w_up, "w_down": w_down}


def round_trip(values):
    return lax.optimization_barrier(values.astype(jnp.bfloat16)).astype(jnp.float32)


def route_tables(expert_ids, gate_weights):
    experts = jnp.arange(EXPERTS, dtype=jnp.int32)
    match = (expert_ids[..., None] == experts).astype(jnp.float32)
    hits = jnp.sum(match, axis=-2)
    chosen = jnp.sum(match * gate_weights[..., None], axis=-2)
    slots = jnp.cumsum(hits, axis=-2) - 1.0
    levels = jnp.arange(CAP, dtype=jnp.float32)
    place = hits[..., None] * (slots[..., None] == levels).astype(jnp.float32)
    return place, chosen


def expert_pass(slot_rows, scaled, gate_cols, up_cols, down_rows):
    width = slot_rows.shape[1]
    gate_pre = jnp.dot(slot_rows, gate_cols, preferred_element_type=jnp.float32)
    up_pre = jnp.dot(slot_rows, up_cols, preferred_element_type=jnp.float32)
    sigma = jax.nn.sigmoid(gate_pre)
    active = gate_pre * sigma
    hidden = (active * up_pre).astype(jnp.bfloat16)
    hidden_parts = hidden.reshape(-1, GROUP, HE_DEV).astype(jnp.float32)
    down_parts = down_rows.reshape(GROUP, HE_DEV, width).astype(jnp.float32)
    out_parts = jnp.einsum('rmk,mkd->mrd', hidden_parts, down_parts)
    expert_out = jnp.sum(round_trip(out_parts), axis=0)
    dhidden = jnp.dot(scaled, down_rows.T, preferred_element_type=jnp.float32)
    dgate = (dhidden * up_pre * sigma * (1.0 + gate_pre * (1.0 - sigma))).astype(jnp.bfloat16)
    dup = (dhidden * active).astype(jnp.bfloat16)
    gate_parts = gate_cols.reshape(width, GROUP, HE_DEV).astype(jnp.float32)
    up_parts = up_cols.reshape(width, GROUP, HE_DEV).astype(jnp.float32)
    dx_parts = jnp.einsum('rmk,dmk->mrd', dgate.reshape(-1, GROUP, HE_DEV).astype(jnp.float32), gate_parts)
    dx_parts = dx_parts + jnp.einsum('rmk,dmk->mrd', dup.reshape(-1, GROUP, HE_DEV).astype(jnp.float32), up_parts)
    dx_rows = jnp.sum(round_trip(dx_parts), axis=0)
    grad_g = jnp.dot(slot_rows.T, dgate, preferred_element_type=jnp.float32)
    grad_u = jnp.dot(slot_rows.T, dup, preferred_element_type=jnp.float32)
    grad_d = jnp.dot(hidden.T, scaled, preferred_element_type=jnp.float32)
    return expert_out, dx_rows, grad_g, grad_u, grad_d


def rank_pass(rank_tokens, rank_cot, rank_ids, rank_gates, gate_full, up_full, down_full):
    place, chosen = route_tables(rank_ids, rank_gates)
    highest = lax.Precision.HIGHEST
    tok_f = rank_tokens.astype(jnp.float32)
    cot_f = rank_cot.astype(jnp.float32)
    rows_all = jnp.einsum('ntec,ntd->encd', place, tok_f, precision=highest).astype(jnp.bfloat16)
    gate_slot = jnp.einsum('ntec,nte->enc', place, chosen, precision=highest)
    raw_cot = jnp.einsum('ntec,ntd->encd', place, cot_f, precision=highest)
    scaled_all = (gate_slot[..., None] * raw_cot).astype(jnp.bfloat16)
    blocks = rank_tokens.shape[0]
    mixed = jnp.zeros(rank_tokens.shape, jnp.float32)
    dinput = jnp.zeros(rank_tokens.shape, jnp.float32)
    grads_g, grads_u, grads_d = [], [], []
    for expert in range(EXPERTS):
        lower = expert * HE
        result = expert_pass(rows_all[expert].reshape(blocks * CAP, D), scaled_all[expert].reshape(blocks * CAP, D),
                             gate_full[:, lower:lower + HE], up_full[:, lower:lower + HE], down_full[lower:lower + HE, :])
        expert_out, dx_rows, grad_g, grad_u, grad_d = result
        weighted = gate_slot[expert][..., None] * expert_out.reshape(blocks, CAP, D)
        mixed = mixed + jnp.einsum('ntc,ncd->ntd', place[:, :, expert, :], weighted, precision=highest)
        dinput = dinput + jnp.einsum('ntc,ncd->ntd', place[:, :, expert, :], dx_rows.reshape(blocks, CAP, D), precision=highest)
        grads_g.append(grad_g)
        grads_u.append(grad_u)
        grads_d.append(grad_d)
    return (mixed.astype(jnp.bfloat16), dinput.astype(jnp.bfloat16), jnp.concatenate(grads_g, axis=1),
            jnp.concatenate(grads_u, axis=1), jnp.concatenate(grads_d, axis=0))


def reference(tokens, cotangent, expert_ids, gate_weights, w_gate, w_up, w_down):
    half_pipe = N_PIPE // 2
    token_blocks = tokens.reshape(N_PIPE, N_EXPERT, TOK_DEV, D)
    cot_blocks = cotangent.reshape(N_PIPE, N_EXPERT, TOK_DEV, D)
    id_blocks = expert_ids.reshape(N_PIPE, N_EXPERT, TOK_DEV, TOP)
    gate_blocks = gate_weights.reshape(N_PIPE, N_EXPERT, TOK_DEV, TOP)

    def pair_pass(pair_index):
        front = pair_index
        back = N_PIPE - 1 - pair_index
        gate_full = jnp.concatenate([w_gate[front], w_gate[back]], axis=0)
        up_full = jnp.concatenate([w_up[front], w_up[back]], axis=0)
        down_full = jnp.concatenate([w_down[front], w_down[back]], axis=1)
        front_res = rank_pass(token_blocks[front], cot_blocks[front], id_blocks[front], gate_blocks[front], gate_full, up_full, down_full)
        back_res = rank_pass(token_blocks[back], cot_blocks[back], id_blocks[back], gate_blocks[back], gate_full, up_full, down_full)
        sum_g = round_trip(front_res[2]) + round_trip(back_res[2])
        sum_u = round_trip(front_res[3]) + round_trip(back_res[3])
        sum_d = round_trip(front_res[4]) + round_trip(back_res[4])
        return (front_res[0], back_res[0], front_res[1], back_res[1],
                sum_g[:D2].astype(jnp.bfloat16), sum_g[D2:].astype(jnp.bfloat16),
                sum_u[:D2].astype(jnp.bfloat16), sum_u[D2:].astype(jnp.bfloat16),
                sum_d[:, :D2].astype(jnp.bfloat16), sum_d[:, D2:].astype(jnp.bfloat16))

    mapped = lax.map(pair_pass, jnp.arange(half_pipe, dtype=jnp.int32))

    def assemble(front_stack, back_stack):
        return jnp.concatenate([front_stack, back_stack[::-1]], axis=0)

    mixed_out = assemble(mapped[0], mapped[1]).reshape(TOKENS, D)
    input_grad = assemble(mapped[2], mapped[3]).reshape(TOKENS, D)
    grad_gate = assemble(mapped[4], mapped[5])
    grad_up = assemble(mapped[6], mapped[7])
    grad_down = assemble(mapped[8], mapped[9])
    return mixed_out, input_grad, grad_gate, grad_up, grad_down
```

```python
import functools

import jax
import jax.numpy as jnp
from jax import lax
from jax.experimental import pallas as pl
from jax.experimental.pallas import tpu as pltpu
from jax.sharding import PartitionSpec as P

GROUP = 8
CAP = 8
NY = 4
NX = 4
STAGES = 4
TILE = 512
MESH = pl.DeviceIdType.MESH
F32 = jnp.float32
BF16 = jnp.bfloat16


def route_tables(expert_ids, gate_weights, flight):
    experts = jnp.arange(flight, dtype=jnp.int32)
    match = (expert_ids[:, :, None] == experts).astype(F32)
    hits = jnp.sum(match, axis=1)
    chosen = jnp.sum(match * gate_weights[:, :, None], axis=1)
    slots = jnp.cumsum(hits, axis=0) - 1.0
    levels = jnp.arange(CAP, dtype=F32)
    place = hits.T[:, None, :] * (slots.T[:, None, :] == levels[None, :, None]).astype(F32)
    return place, chosen


def dot(a, b):
    return jnp.dot(a, b, preferred_element_type=F32)


def loop(n, body):
    def step(i, carry):
        body(i)
        return carry

    lax.fori_loop(0, n, step, 0)


def kernel(
    tok_hbm, cot_hbm, place_hbm, gsl_hbm, wg_hbm, wu_hbm, wd_hbm,
    mixed_hbm, igrad_hbm, gg_hbm, gu_hbm, gd_hbm,
    tok, cot, place, gsl, wgu, wguT, wd, wdT, sb, xs, x2d, s2d, part, pbs, pbr,
    h16, dgu16, ob, mid, rb, fb, mixed, igrad, gg, gu, gd,
    in_sem, out_sem, zsend, xsend, xfsend, recv, psend, precv, msend, mrecv, rsend, rrecv, osend, orecv,
):
    half = wd.shape[1]
    tiles = half // TILE
    p = lax.axis_index("pipe")
    e = lax.axis_index("expert")
    y = lax.div(e, 8)
    zh = lax.rem(lax.div(e, 4), 2)
    x = lax.rem(e, 4)
    h = lax.div(p, 4)
    q = p + h * (7 - 2 * p)
    right = lax.rem(x + 1, 4)
    left = lax.rem(x + 3, 4)
    across = lax.rem(x + 2, 4)
    yz = e - x

    def rank_of(hh):
        return q + hh * (7 - 2 * q)

    def flip(i):
        return lax.rem(lax.div(i, 2) + lax.div(q, 2), 2) * 2 + lax.rem(lax.rem(i, 2) + lax.rem(q, 2), 2)

    own_s = (h * 2 + zh) * 4 + y
    own_stage = flip(h * 2 + zh)

    def remote(src, dst, ssem, rsem, rank, expert):
        return pltpu.make_async_remote_copy(
            src_ref=src, dst_ref=dst, send_sem=ssem, recv_sem=rsem,
            device_id=(rank, expert), device_id_type=MESH)

    def arrived(ref, sem):
        pltpu.make_async_copy(ref, ref, sem).wait()

    def peer(t):
        j, d = lax.div(t, 4), lax.rem(t, 4)
        hh = lax.rem(h + lax.div(d, 2), 2)
        zz = lax.rem(zh + lax.rem(d, 2), 2)
        yy = lax.rem(y + 4 - j, 4)
        return hh, zz, yy

    barrier = pltpu.get_barrier_semaphore()

    def greet(t):
        hh, zz, yy = peer(t + 1)
        pl.semaphore_signal(barrier, inc=1, device_id=(rank_of(hh), yy * 8 + zz * 4 + x), device_id_type=MESH)

    loop(15, greet)
    pl.semaphore_signal(barrier, inc=1, device_id=(p, yz + right), device_id_type=MESH)
    pl.semaphore_signal(barrier, inc=1, device_id=(p, yz + left), device_id_type=MESH)

    loads = [
        pltpu.make_async_copy(place_hbm, place, in_sem.at[0]),
        pltpu.make_async_copy(gsl_hbm, gsl, in_sem.at[1]),
        pltpu.make_async_copy(tok_hbm, tok, in_sem.at[2]),
        pltpu.make_async_copy(cot_hbm, cot, in_sem.at[3]),
        pltpu.make_async_copy(wg_hbm, wgu.at[:, pl.ds(0, 128)], in_sem.at[4]),
        pltpu.make_async_copy(wu_hbm, wgu.at[:, pl.ds(128, 128)], in_sem.at[5]),
        pltpu.make_async_copy(wd_hbm, wd, in_sem.at[6]),
    ]
    for load in loads:
        load.start()
    for load in loads[:4]:
        load.wait()

    def slot_rows(ct):
        hf, col = lax.div(ct, tiles), lax.rem(ct, tiles) * TILE
        cols = pl.ds(pl.multiple_of(ct * TILE, TILE), TILE)
        to = pl.ds(pl.multiple_of(col, TILE), TILE)
        rows = dot(place[...], tok[:, cols])
        sb[:, hf, 0, :, to] = rows.reshape(NY, CAP, TILE).astype(BF16)
        raw = dot(place[...], cot[:, cols]) * gsl[...]
        sb[:, hf, 1, :, to] = raw.reshape(NY, CAP, TILE).astype(BF16)

    loop(2 * tiles, slot_rows)
    pl.semaphore_wait(barrier, 17)

    local = pltpu.make_async_copy(sb.at[y, h], xs.at[x, own_s], recv.at[x, own_s])

    def zcopy(t):
        hh, zz, yy = peer(t)
        return remote(sb.at[yy, hh], xs.at[x, own_s], zsend.at[t], recv.at[x, own_s],
                      rank_of(hh), yy * 8 + zz * 4 + x)

    def send_out(stage):
        @pl.when(own_stage == stage)
        def _():
            local.start()
            loop(15, lambda t: zcopy(t + 1).start())

    def source(i, j):
        return flip(i) * 4 + lax.rem(y + j, 4)

    def xcopy(s, side):
        return remote(xs.at[x, s], xs.at[x, s], xsend.at[side, s], recv.at[x, s],
                      p, yz + (right if side == 0 else left))

    def xforward(s):
        odd = lax.rem(s, 2)
        c = lax.rem(x + 3 + 2 * odd, 4)
        to = lax.rem(x + 1 + 2 * odd, 4)
        return remote(xs.at[c, s], xs.at[c, s], xfsend.at[s], recv.at[c, s], p, yz + to)

    def gather_own(i):
        def one(j):
            s = source(i, j)
            arrived(xs.at[x, s], recv.at[x, s])
            xcopy(s, 0).start()
            xcopy(s, 1).start()

        loop(4, one)

    def gather_forward(i):
        def one(j):
            s = source(i, j)
            c = lax.rem(x + 3 + 2 * lax.rem(s, 2), 4)
            arrived(xs.at[c, s], recv.at[c, s])
            xforward(s).start()

        loop(4, one)

    def gather_rest(i):
        def one(j):
            s = source(i, j)
            c = lax.rem(x + 1 + 2 * lax.rem(s, 2), 4)
            arrived(xs.at[c, s], recv.at[c, s])
            arrived(xs.at[across, s], recv.at[across, s])

        loop(4, one)

    def pcopy(i):
        return remote(pbs.at[i], pbr.at[i], psend.at[i], precv.at[i], 7 - p, e)

    def rows_of(i):
        return pl.ds(pl.multiple_of(i * 128, 128), 128)

    def first_dots(i):
        g4 = flip(i) * 4

        def flatten(c):
            to = pl.ds(pl.multiple_of(i * 128 + c * 32, 32), 32)
            x2d[to, :] = xs[c, pl.ds(g4, 4), 0].astype(F32).reshape(32, half).astype(BF16)
            s2d[to, :] = xs[c, pl.ds(g4, 4), 1].astype(F32).reshape(32, half).astype(BF16)

        loop(4, flatten)
        rows = rows_of(i)
        part[i, :, 0:256] = dot(x2d[rows, :], wgu[...])
        part[i, :, 256:384] = dot(s2d[rows, :], wdT[...])
        pbs[i] = part[i].reshape(16, 8, 384).astype(BF16)
        pcopy(i).start()

    def mid_copy(s):
        to = lax.rem(x + 3 + 2 * lax.rem(s, 2), 4)
        return remote(ob.at[across, s], mid.at[s], msend.at[s], mrecv.at[s], p, yz + to)

    def near_copy(s, side):
        c = left if side == 0 else right
        return remote(ob.at[c, s], rb.at[side, s], rsend.at[side, s], rrecv.at[side, s], p, yz + c)

    def near_copy_by(s, side):
        c = lax.rem(x + 3 + 2 * side, 4)
        return remote(ob.at[c, s], rb.at[side, s], rsend.at[side, s], rrecv.at[side, s], p, yz + c)

    def second_dots(i):
        g4 = flip(i) * 4
        rows = rows_of(i)
        arrived(pbr.at[i], precv.at[i])
        whole = part[i] + pbr[i].astype(F32).reshape(128, 384)
        gate, up, dh = whole[:, 0:128], whole[:, 128:256], whole[:, 256:384]
        sigma = jax.nn.sigmoid(gate)
        active = gate * sigma
        h16[rows, :] = (active * up).astype(BF16)
        dgu16[rows, 0:128] = (dh * up * sigma * (1.0 + gate * (1.0 - sigma))).astype(BF16)
        dgu16[rows, 128:256] = (dh * active).astype(BF16)

        def tile(ct):
            cols = pl.ds(pl.multiple_of(ct * TILE, TILE), TILE)
            out = dot(h16[rows, :], wd[:, cols])
            ob[:, pl.ds(g4, 4), 0, :, cols] = out.reshape(NX, NY, CAP, TILE).astype(BF16)
            back = dot(dgu16[rows, :], wguT[:, cols])
            ob[:, pl.ds(g4, 4), 1, :, cols] = back.reshape(NX, NY, CAP, TILE).astype(BF16)

        loop(tiles, tile)
        loop(4, lambda j: mid_copy(source(i, j)).start())

        def direct(j):
            s = source(i, j)
            near_copy_by(s, 1 - lax.rem(s, 2)).start()

        loop(4, direct)

    def add_mid(i):
        def one(j):
            s = source(i, j)
            odd = lax.rem(s, 2)
            c = lax.rem(x + 3 + 2 * odd, 4)
            arrived(mid.at[s], mrecv.at[s])
            ob[c, s] = (ob[c, s].astype(F32) + mid[s].astype(F32)).astype(BF16)
            near_copy_by(s, odd).start()

        loop(4, one)

    def owner_copy(s):
        g = lax.div(s, 4)
        return remote(ob.at[x, s], fb.at[y, h, zh], osend.at[s], orecv.at[(y * 2 + h) * 2 + zh],
                      rank_of(lax.div(g, 2)), lax.rem(s, 4) * 8 + lax.rem(g, 2) * 4 + x)

    own_out = pltpu.make_async_copy(ob.at[x, own_s], fb.at[y, h, zh], orecv.at[(y * 2 + h) * 2 + zh])

    def add_last(i):
        def one(j):
            s = source(i, j)
            arrived(rb.at[0, s], rrecv.at[0, s])
            arrived(rb.at[1, s], rrecv.at[1, s])
            ob[x, s] = (ob[x, s].astype(F32) + rb[0, s].astype(F32) + rb[1, s].astype(F32)).astype(BF16)

            @pl.when(s == own_s)
            def _():
                own_out.start()

            @pl.when(s != own_s)
            def _():
                owner_copy(s).start()

        loop(4, one)

    send_out(0)
    send_out(1)
    for load in loads[4:]:
        load.wait()

    def turn(ct):
        cols = pl.ds(pl.multiple_of(ct * TILE, TILE), TILE)
        wguT[:, cols] = wgu[cols, :].T
        wdT[cols, :] = wd[:, cols].T

    loop(tiles, turn)
    gather_own(0)

    def weight_grads():
        dguT = dgu16[...].T
        hT = h16[...].T

        def tile(ct):
            cols = pl.ds(pl.multiple_of(ct * TILE, TILE), TILE)
            both = dot(dguT, x2d[:, cols]).T
            gg[cols, :] = both[:, 0:128].astype(BF16)
            gu[cols, :] = both[:, 128:256].astype(BF16)
            gd[:, cols] = dot(hT, s2d[:, cols]).astype(BF16)

        loop(tiles, tile)

    def turn_of(i):
        @pl.when(i < 2)
        def _():
            send_out(i + 2)

        @pl.when(i < 4)
        def _():
            gather_forward(i)

        @pl.when(i < 3)
        def _():
            gather_own(i + 1)

        @pl.when(i < 4)
        def _():
            gather_rest(i)
            first_dots(i)

        @pl.when(i >= 2)
        def _():
            add_mid(i - 2)

        @pl.when(jnp.logical_and(i >= 1, i < 5))
        def _():
            second_dots(i - 1)

        @pl.when(i >= 2)
        def _():
            add_last(i - 2)

        @pl.when(i == 4)
        def _():
            weight_grads()

    loop(6, turn_of)

    stores = [
        pltpu.make_async_copy(gg, gg_hbm, out_sem.at[0]),
        pltpu.make_async_copy(gu, gu_hbm, out_sem.at[1]),
        pltpu.make_async_copy(gd, gd_hbm, out_sem.at[2]),
        pltpu.make_async_copy(mixed, mixed_hbm, out_sem.at[3]),
        pltpu.make_async_copy(igrad, igrad_hbm, out_sem.at[4]),
    ]
    for store in stores[:3]:
        store.start()

    def landed(t):
        k, hz = lax.div(t, 4), lax.rem(t, 4)
        hh, zz = lax.div(hz, 2), lax.rem(hz, 2)
        arrived(fb.at[k, hh, zz], orecv.at[t])

    loop(16, landed)

    placeT = place[...].T

    def combine(ct):
        hf, col = lax.div(ct, tiles), lax.rem(ct, tiles) * TILE
        cols = pl.ds(pl.multiple_of(ct * TILE, TILE), TILE)
        fr = pl.ds(pl.multiple_of(col, TILE), TILE)

        def both(k):
            return (fb[:, hf, 0, k, :, fr].astype(F32) + fb[:, hf, 1, k, :, fr].astype(F32)).reshape(32, TILE)

        mixed[:, cols] = dot(placeT, (both(0) * gsl[...]).astype(BF16)).astype(BF16)
        igrad[:, cols] = dot(placeT, both(1).astype(BF16)).astype(BF16)

    loop(2 * tiles, combine)
    for store in stores[3:]:
        store.start()

    loop(15, lambda t: zcopy(t + 1).wait_send())

    def sent(s):
        xcopy(s, 0).wait_send()
        xcopy(s, 1).wait_send()
        xforward(s).wait_send()
        mid_copy(s).wait_send()
        near_copy(s, 0).wait_send()
        near_copy(s, 1).wait_send()

        @pl.when(s != own_s)
        def _():
            owner_copy(s).wait_send()

    loop(16, sent)
    loop(STAGES, lambda i: pcopy(i).wait_send())
    for store in stores:
        store.wait()


def per_device(tokens, cotangent, expert_ids, gate_weights, w_gate, w_up, w_down):
    flight = lax.axis_size("expert") // GROUP
    tok_count, width = tokens.shape
    half = width // 2
    highest = lax.Precision.HIGHEST
    place, chosen = route_tables(expert_ids, gate_weights, flight)
    gate_slot = jnp.einsum("ect,te->ec", place, chosen, precision=highest).reshape(-1, 1)
    place16 = place.reshape(flight * CAP, tok_count).astype(BF16)
    dma = pltpu.SemaphoreType.DMA
    vmem = pltpu.VMEM
    piece = (2, CAP, half)
    any_spec = pl.BlockSpec(memory_space=pl.ANY)
    outs = pl.pallas_call(
        kernel,
        out_shape=(
            jax.ShapeDtypeStruct((tok_count, width), BF16),
            jax.ShapeDtypeStruct((tok_count, width), BF16),
            jax.ShapeDtypeStruct((half, 128), BF16),
            jax.ShapeDtypeStruct((half, 128), BF16),
            jax.ShapeDtypeStruct((128, half), BF16),
        ),
        in_specs=[any_spec] * 7,
        out_specs=[any_spec] * 5,
        scratch_shapes=[
            vmem((tok_count, width), BF16),
            vmem((tok_count, width), BF16),
            vmem((32, tok_count), BF16),
            vmem((32, 1), F32),
            vmem((half, 256), BF16),
            vmem((256, half), BF16),
            vmem((128, half), BF16),
            vmem((half, 128), BF16),
            vmem((NY, 2) + piece, BF16),
            vmem((NX, 16) + piece, BF16),
            vmem((512, half), BF16),
            vmem((512, half), BF16),
            vmem((STAGES, 128, 384), F32),
            vmem((STAGES, 16, 8, 384), BF16),
            vmem((STAGES, 16, 8, 384), BF16),
            vmem((512, 128), BF16),
            vmem((512, 256), BF16),
            vmem((NX, 16) + piece, BF16),
            vmem((16,) + piece, BF16),
            vmem((2, 16) + piece, BF16),
            vmem((NY, 2, 2) + piece, BF16),
            vmem((tok_count, width), BF16),
            vmem((tok_count, width), BF16),
            vmem((half, 128), BF16),
            vmem((half, 128), BF16),
            vmem((128, half), BF16),
            dma((7,)),
            dma((5,)),
            dma((16,)),
            dma((2, 16)),
            dma((16,)),
            dma((NX, 16)),
            dma((STAGES,)),
            dma((STAGES,)),
            dma((16,)),
            dma((16,)),
            dma((2, 16)),
            dma((2, 16)),
            dma((16,)),
            dma((16,)),
        ],
        compiler_params=pltpu.CompilerParams(
            collective_id=0, has_side_effects=True, vmem_limit_bytes=60 * 1024 * 1024
        ),
    )(tokens, cotangent, place16, gate_slot, w_gate[0], w_up[0], w_down[0])
    return outs[0], outs[1], outs[2][None], outs[3][None], outs[4][None]


def solution(mesh):
    return jax.shard_map(
        per_device,
        mesh=mesh,
        in_specs=(
            P(("pipe", "expert"), None),
            P(("pipe", "expert"), None),
            P(("pipe", "expert"), None),
            P(("pipe", "expert"), None),
            P("pipe", None, "expert"),
            P("pipe", None, "expert"),
            P("pipe", "expert", None),
        ),
        out_specs=(
            P(("pipe", "expert"), None),
            P(("pipe", "expert"), None),
            P("pipe", None, "expert"),
            P("pipe", None, "expert"),
            P("pipe", "expert", None),
        ),
        check_vma=False,
    )
```

```python
import functools

import jax
import jax.numpy as jnp
from jax import lax
from jax.experimental import pallas as pl
from jax.experimental.pallas import tpu as pltpu
from jax.sharding import PartitionSpec as P

CAP = 8
NY = 4
NX = 4
STAGES = 4
TILE = 512
MESH = pl.DeviceIdType.MESH
F32 = jnp.float32
BF16 = jnp.bfloat16


def route(ids, gates):
    count = ids.shape[1]
    hits, chosen = [], []
    for expert in range(NY):
        match = ids == expert
        hits.append(jnp.sum(match.astype(F32), axis=0, keepdims=True))
        chosen.append(jnp.sum(jnp.where(match, gates, 0.0), axis=0, keepdims=True))
    tri = lax.broadcasted_iota(jnp.int32, (count, count), 0) <= lax.broadcasted_iota(jnp.int32, (count, count), 1)
    stacked = jnp.concatenate([jnp.broadcast_to(hit, (CAP, count)) for hit in hits], axis=0)
    slots = dot(stacked.astype(BF16), tri.astype(F32).astype(BF16)) - 1.0
    level = lax.rem(lax.broadcasted_iota(jnp.int32, (NY * CAP, count), 0), CAP).astype(F32)
    place = jnp.where(slots == level, stacked, 0.0)
    gate = jnp.concatenate([jnp.broadcast_to(row, (CAP, count)) for row in chosen], axis=0)
    return place, jnp.sum(place * gate, axis=1, keepdims=True)


def dot(a, b):
    return jnp.dot(a, b, preferred_element_type=F32)


def loop(n, body):
    def step(i, carry):
        body(i)
        return carry

    lax.fori_loop(0, n, step, 0)


def kernel(
    tok_hbm, cot_hbm, ids_hbm, gates_hbm, wg_hbm, wu_hbm, wd_hbm,
    fb, gg_hbm, gu_hbm, gd_hbm,
    tok, cot, ids, gates, place, gsl, wgu, wguT, wd, wdT, sb, xs, x2d, s2d, part, pbs, pbr,
    h16, dgu16, ob, mid, rb, gg, gu, gd,
    in_sem, out_sem, zsend, xsend, xfsend, recv, psend, precv, msend, mrecv, rsend, rrecv, osend, orecv,
):
    half = wd.shape[1]
    tiles = half // TILE
    p = lax.axis_index("pipe")
    e = lax.axis_index("expert")
    y = lax.div(e, 8)
    zh = lax.rem(lax.div(e, 4), 2)
    x = lax.rem(e, 4)
    h = lax.div(p, 4)
    q = p + h * (7 - 2 * p)
    right = lax.rem(x + 1, 4)
    left = lax.rem(x + 3, 4)
    across = lax.rem(x + 2, 4)
    yz = e - x

    def rank_of(hh):
        return q + hh * (7 - 2 * q)

    def flip(i):
        return lax.rem(lax.div(i, 2) + lax.div(q, 2), 2) * 2 + lax.rem(lax.rem(i, 2) + lax.rem(q, 2), 2)

    own_s = (h * 2 + zh) * 4 + y
    own_stage = flip(h * 2 + zh)

    def remote(src, dst, ssem, rsem, rank, expert):
        return pltpu.make_async_remote_copy(
            src_ref=src, dst_ref=dst, send_sem=ssem, recv_sem=rsem,
            device_id=(rank, expert), device_id_type=MESH)

    def arrived(ref, sem):
        pltpu.make_async_copy(ref, ref, sem).wait()

    def peer(t):
        j, d = lax.div(t, 4), lax.rem(t, 4)
        hh = lax.rem(h + lax.div(d, 2), 2)
        zz = lax.rem(zh + lax.rem(d, 2), 2)
        yy = lax.rem(y + 4 - j, 4)
        return hh, zz, yy

    barrier = pltpu.get_barrier_semaphore()

    def greet(t):
        hh, zz, yy = peer(t + 1)
        pl.semaphore_signal(barrier, inc=1, device_id=(rank_of(hh), yy * 8 + zz * 4 + x), device_id_type=MESH)

    loop(15, greet)
    pl.semaphore_signal(barrier, inc=1, device_id=(p, yz + right), device_id_type=MESH)
    pl.semaphore_signal(barrier, inc=1, device_id=(p, yz + left), device_id_type=MESH)

    loads = [
        pltpu.make_async_copy(ids_hbm, ids, in_sem.at[0]),
        pltpu.make_async_copy(gates_hbm, gates, in_sem.at[1]),
        pltpu.make_async_copy(tok_hbm, tok, in_sem.at[2]),
        pltpu.make_async_copy(cot_hbm, cot, in_sem.at[3]),
        pltpu.make_async_copy(wg_hbm, wgu.at[:, pl.ds(0, 128)], in_sem.at[4]),
        pltpu.make_async_copy(wu_hbm, wgu.at[:, pl.ds(128, 128)], in_sem.at[5]),
        pltpu.make_async_copy(wd_hbm, wd, in_sem.at[6]),
    ]
    for load in loads:
        load.start()
    for load in loads[:2]:
        load.wait()
    placed, gate_slot = route(ids[...], gates[...])
    place[...] = placed.astype(BF16)
    gsl[...] = gate_slot
    for load in loads[2:4]:
        load.wait()

    def slot_rows(ct):
        hf, col = lax.div(ct, tiles), lax.rem(ct, tiles) * TILE
        cols = pl.ds(pl.multiple_of(ct * TILE, TILE), TILE)
        to = pl.ds(pl.multiple_of(col, TILE), TILE)
        rows = dot(place[...], tok[:, cols])
        sb[:, hf, 0, :, to] = rows.reshape(NY, CAP, TILE).astype(BF16)
        raw = dot(place[...], cot[:, cols]) * gsl[...]
        sb[:, hf, 1, :, to] = raw.reshape(NY, CAP, TILE).astype(BF16)

    loop(2 * tiles, slot_rows)
    pl.semaphore_wait(barrier, 17)

    local = pltpu.make_async_copy(sb.at[y, h], xs.at[x, own_s], recv.at[x, own_s])

    def zcopy(t):
        hh, zz, yy = peer(t)
        return remote(sb.at[yy, hh], xs.at[x, own_s], zsend.at[t], recv.at[x, own_s],
                      rank_of(hh), yy * 8 + zz * 4 + x)

    def send_out(stage):
        @pl.when(own_stage == stage)
        def _():
            local.start()
            loop(15, lambda t: zcopy(t + 1).start())

    def source(i, j):
        return flip(i) * 4 + lax.rem(y + j, 4)

    def xcopy(s, side):
        return remote(xs.at[x, s], xs.at[x, s], xsend.at[side, s], recv.at[x, s],
                      p, yz + (right if side == 0 else left))

    def xforward(s):
        odd = lax.rem(s, 2)
        c = lax.rem(x + 3 + 2 * odd, 4)
        to = lax.rem(x + 1 + 2 * odd, 4)
        return remote(xs.at[c, s], xs.at[c, s], xfsend.at[s], recv.at[c, s], p, yz + to)

    def gather_own(i):
        def one(j):
            s = source(i, j)
            arrived(xs.at[x, s], recv.at[x, s])
            xcopy(s, 0).start()
            xcopy(s, 1).start()

        loop(4, one)

    def gather_forward(i):
        def one(j):
            s = source(i, j)
            c = lax.rem(x + 3 + 2 * lax.rem(s, 2), 4)
            arrived(xs.at[c, s], recv.at[c, s])
            xforward(s).start()

        loop(4, one)

    def gather_rest(i):
        def one(j):
            s = source(i, j)
            c = lax.rem(x + 1 + 2 * lax.rem(s, 2), 4)
            arrived(xs.at[c, s], recv.at[c, s])
            arrived(xs.at[across, s], recv.at[across, s])

        loop(4, one)

    def pcopy(i):
        return remote(pbs.at[i], pbr.at[i], psend.at[i], precv.at[i], 7 - p, e)

    def rows_of(i):
        return pl.ds(pl.multiple_of(i * 128, 128), 128)

    def first_dots(i):
        g4 = flip(i) * 4

        def flatten(c):
            to = pl.ds(pl.multiple_of(i * 128 + c * 32, 32), 32)
            x2d[to, :] = xs[c, pl.ds(g4, 4), 0].astype(F32).reshape(32, half).astype(BF16)
            s2d[to, :] = xs[c, pl.ds(g4, 4), 1].astype(F32).reshape(32, half).astype(BF16)

        loop(4, flatten)
        rows = rows_of(i)
        part[i, :, 0:256] = dot(x2d[rows, :], wgu[...])
        part[i, :, 256:384] = dot(s2d[rows, :], wdT[...])
        pbs[i] = part[i].reshape(16, 8, 384).astype(BF16)
        pcopy(i).start()

    def mid_copy(s):
        to = lax.rem(x + 3 + 2 * lax.rem(s, 2), 4)
        return remote(ob.at[across, s], mid.at[s], msend.at[s], mrecv.at[s], p, yz + to)

    def near_copy(s, side):
        c = left if side == 0 else right
        return remote(ob.at[c, s], rb.at[side, s], rsend.at[side, s], rrecv.at[side, s], p, yz + c)

    def near_copy_by(s, side):
        c = lax.rem(x + 3 + 2 * side, 4)
        return remote(ob.at[c, s], rb.at[side, s], rsend.at[side, s], rrecv.at[side, s], p, yz + c)

    def second_dots(i):
        g4 = flip(i) * 4
        rows = rows_of(i)
        arrived(pbr.at[i], precv.at[i])
        whole = part[i] + pbr[i].astype(F32).reshape(128, 384)
        gate, up, dh = whole[:, 0:128], whole[:, 128:256], whole[:, 256:384]
        sigma = jax.nn.sigmoid(gate)
        active = gate * sigma
        h16[rows, :] = (active * up).astype(BF16)
        dgu16[rows, 0:128] = (dh * up * sigma * (1.0 + gate * (1.0 - sigma))).astype(BF16)
        dgu16[rows, 128:256] = (dh * active).astype(BF16)

        def tile(ct):
            cols = pl.ds(pl.multiple_of(ct * TILE, TILE), TILE)
            out = dot(h16[rows, :], wd[:, cols])
            ob[:, pl.ds(g4, 4), 0, :, cols] = out.reshape(NX, NY, CAP, TILE).astype(BF16)
            back = dot(dgu16[rows, :], wguT[:, cols])
            ob[:, pl.ds(g4, 4), 1, :, cols] = back.reshape(NX, NY, CAP, TILE).astype(BF16)

        loop(tiles, tile)
        loop(4, lambda j: mid_copy(source(i, j)).start())

        def direct(j):
            s = source(i, j)
            near_copy_by(s, 1 - lax.rem(s, 2)).start()

        loop(4, direct)

    def add_mid(i):
        def one(j):
            s = source(i, j)
            odd = lax.rem(s, 2)
            c = lax.rem(x + 3 + 2 * odd, 4)
            arrived(mid.at[s], mrecv.at[s])
            ob[c, s] = (ob[c, s].astype(F32) + mid[s].astype(F32)).astype(BF16)
            near_copy_by(s, odd).start()

        loop(4, one)

    def owner_copy(s):
        g = lax.div(s, 4)
        return remote(ob.at[x, s], fb.at[y, h, zh], osend.at[s], orecv.at[(y * 2 + h) * 2 + zh],
                      rank_of(lax.div(g, 2)), lax.rem(s, 4) * 8 + lax.rem(g, 2) * 4 + x)

    own_out = pltpu.make_async_copy(ob.at[x, own_s], fb.at[y, h, zh], orecv.at[(y * 2 + h) * 2 + zh])

    def add_last(i):
        def one(j):
            s = source(i, j)
            arrived(rb.at[0, s], rrecv.at[0, s])
            arrived(rb.at[1, s], rrecv.at[1, s])
            ob[x, s] = (ob[x, s].astype(F32) + rb[0, s].astype(F32) + rb[1, s].astype(F32)).astype(BF16)

            @pl.when(s == own_s)
            def _():
                own_out.start()

            @pl.when(s != own_s)
            def _():
                owner_copy(s).start()

        loop(4, one)

    send_out(0)
    for load in loads[4:]:
        load.wait()

    def turn(ct):
        cols = pl.ds(pl.multiple_of(ct * TILE, TILE), TILE)
        wguT[:, cols] = wgu[cols, :].T
        wdT[cols, :] = wd[:, cols].T

    loop(tiles, turn)
    gather_own(0)
    send_out(1)

    def weight_grads(first, last):
        dguT = dgu16[...].T
        hT = h16[...].T

        def tile(n):
            cols = pl.ds(pl.multiple_of((n + first) * TILE, TILE), TILE)
            both = dot(dguT, x2d[:, cols]).T
            gg[cols, :] = both[:, 0:128].astype(BF16)
            gu[cols, :] = both[:, 128:256].astype(BF16)
            gd[:, cols] = dot(hT, s2d[:, cols]).astype(BF16)

        loop(last - first, tile)

    def turn_of(i):
        @pl.when(i < 4)
        def _():
            gather_forward(i)

        @pl.when(i < 3)
        def _():
            gather_own(i + 1)

        @pl.when(i < 2)
        def _():
            send_out(i + 2)

        @pl.when(i >= 2)
        def _():
            add_mid(i - 2)

        @pl.when(jnp.logical_and(i >= 1, i < 5))
        def _():
            second_dots(i - 1)

        @pl.when(i < 4)
        def _():
            gather_rest(i)
            first_dots(i)

        @pl.when(i == 5)
        def _():
            weight_grads(4, tiles)

        @pl.when(i >= 2)
        def _():
            add_last(i - 2)

        @pl.when(i == 4)
        def _():
            weight_grads(0, 4)

    loop(6, turn_of)

    stores = [
        pltpu.make_async_copy(gg, gg_hbm, out_sem.at[0]),
        pltpu.make_async_copy(gu, gu_hbm, out_sem.at[1]),
        pltpu.make_async_copy(gd, gd_hbm, out_sem.at[2]),
    ]
    for store in stores:
        store.start()

    loop(15, lambda t: zcopy(t + 1).wait_send())

    def sent(s):
        xcopy(s, 0).wait_send()
        xcopy(s, 1).wait_send()
        xforward(s).wait_send()
        mid_copy(s).wait_send()
        near_copy(s, 0).wait_send()
        near_copy(s, 1).wait_send()

        @pl.when(s != own_s)
        def _():
            owner_copy(s).wait_send()

    loop(16, sent)
    loop(STAGES, lambda i: pcopy(i).wait_send())

    def landed(t):
        k, hz = lax.div(t, 4), lax.rem(t, 4)
        hh, zz = lax.div(hz, 2), lax.rem(hz, 2)
        arrived(fb.at[k, hh, zz], orecv.at[t])

    loop(16, landed)
    for store in stores:
        store.wait()


def finish(
    ids_ref, gates_ref, fb_hbm, gg_in, gu_in, gd_in, mixed_hbm, igrad_hbm, gg_out, gu_out, gd_out,
    fb, mixed, igrad, gg, gu, gd, in_sem, out_sem, pass_sem,
):
    half = fb.shape[-1]
    grads = ((gg_in, gg, gg_out), (gu_in, gu, gu_out), (gd_in, gd, gd_out))
    enter = [pltpu.make_async_copy(grad[0], grad[1], pass_sem.at[0, n]) for n, grad in enumerate(grads)]
    leave = [pltpu.make_async_copy(grad[1], grad[2], pass_sem.at[1, n]) for n, grad in enumerate(grads)]
    fetch = [pltpu.make_async_copy(fb_hbm.at[:, hf], fb.at[:, hf], in_sem.at[hf]) for hf in range(2)]
    for copy in fetch + enter:
        copy.start()
    place, gsl = route(ids_ref[...], gates_ref[...])
    placeT = place.T.astype(BF16)
    stores = []
    for hf in range(2):
        fetch[hf].wait()
        for col in range(0, half, TILE):
            fr, to = pl.ds(col, TILE), pl.ds(hf * half + col, TILE)

            def both(k):
                return (fb[:, hf, 0, k, :, fr].astype(F32) + fb[:, hf, 1, k, :, fr].astype(F32)).reshape(32, TILE)

            mixed[:, to] = dot(placeT, (both(0) * gsl).astype(BF16)).astype(BF16)
            igrad[:, to] = dot(placeT, both(1).astype(BF16)).astype(BF16)
        if hf == 0:
            for get, put in zip(enter, leave):
                get.wait()
                put.start()
        cols = pl.ds(hf * half, half)
        stores += [
            pltpu.make_async_copy(mixed.at[:, cols], mixed_hbm.at[:, cols], out_sem.at[hf, 0]),
            pltpu.make_async_copy(igrad.at[:, cols], igrad_hbm.at[:, cols], out_sem.at[hf, 1]),
        ]
        stores[-2].start()
        stores[-1].start()
    for copy in stores + leave:
        copy.wait()


def per_device(tokens, cotangent, expert_ids, gate_weights, w_gate, w_up, w_down):
    tok_count, width = tokens.shape
    half = width // 2
    ids, gates = expert_ids.T, gate_weights.T
    dma = pltpu.SemaphoreType.DMA
    vmem = pltpu.VMEM
    piece = (2, CAP, half)
    any_spec = pl.BlockSpec(memory_space=pl.ANY)
    outs = pl.pallas_call(
        kernel,
        out_shape=(
            jax.ShapeDtypeStruct((NY, 2, 2) + piece, BF16),
            jax.ShapeDtypeStruct((half, 128), BF16),
            jax.ShapeDtypeStruct((half, 128), BF16),
            jax.ShapeDtypeStruct((128, half), BF16),
        ),
        in_specs=[any_spec] * 7,
        out_specs=[any_spec] * 4,
        scratch_shapes=[
            vmem((tok_count, width), BF16),
            vmem((tok_count, width), BF16),
            vmem(ids.shape, jnp.int32),
            vmem(gates.shape, F32),
            vmem((32, tok_count), BF16),
            vmem((32, 1), F32),
            vmem((half, 256), BF16),
            vmem((256, half), BF16),
            vmem((128, half), BF16),
            vmem((half, 128), BF16),
            vmem((NY, 2) + piece, BF16),
            vmem((NX, 16) + piece, BF16),
            vmem((512, half), BF16),
            vmem((512, half), BF16),
            vmem((STAGES, 128, 384), F32),
            vmem((STAGES, 16, 8, 384), BF16),
            vmem((STAGES, 16, 8, 384), BF16),
            vmem((512, 128), BF16),
            vmem((512, 256), BF16),
            vmem((NX, 16) + piece, BF16),
            vmem((16,) + piece, BF16),
            vmem((2, 16) + piece, BF16),
            vmem((half, 128), BF16),
            vmem((half, 128), BF16),
            vmem((128, half), BF16),
            dma((7,)),
            dma((3,)),
            dma((16,)),
            dma((2, 16)),
            dma((16,)),
            dma((NX, 16)),
            dma((STAGES,)),
            dma((STAGES,)),
            dma((16,)),
            dma((16,)),
            dma((2, 16)),
            dma((2, 16)),
            dma((16,)),
            dma((16,)),
        ],
        compiler_params=pltpu.CompilerParams(
            collective_id=0, has_side_effects=True, vmem_limit_bytes=60 * 1024 * 1024
        ),
    )(tokens, cotangent, ids, gates, w_gate[0], w_up[0], w_down[0])
    whole = pl.BlockSpec(memory_space=vmem)
    mixed, igrad, gg, gu, gd = pl.pallas_call(
        finish,
        out_shape=(
            jax.ShapeDtypeStruct((tok_count, width), BF16),
            jax.ShapeDtypeStruct((tok_count, width), BF16),
            jax.ShapeDtypeStruct((half, 128), BF16),
            jax.ShapeDtypeStruct((half, 128), BF16),
            jax.ShapeDtypeStruct((128, half), BF16),
        ),
        in_specs=[whole] * 2 + [any_spec] * 4,
        out_specs=[any_spec] * 5,
        scratch_shapes=[
            vmem((NY, 2, 2) + piece, BF16),
            vmem((tok_count, width), BF16),
            vmem((tok_count, width), BF16),
            vmem((half, 128), BF16),
            vmem((half, 128), BF16),
            vmem((128, half), BF16),
            dma((2,)),
            dma((2, 2)),
            dma((2, 3)),
        ],
        compiler_params=pltpu.CompilerParams(vmem_limit_bytes=60 * 1024 * 1024),
    )(ids, gates, *outs)
    return mixed, igrad, gg[None], gu[None], gd[None]


def solution(mesh):
    return jax.shard_map(
        per_device,
        mesh=mesh,
        in_specs=(
            P(("pipe", "expert"), None),
            P(("pipe", "expert"), None),
            P(("pipe", "expert"), None),
            P(("pipe", "expert"), None),
            P("pipe", None, "expert"),
            P("pipe", None, "expert"),
            P("pipe", "expert", None),
        ),
        out_specs=(
            P(("pipe", "expert"), None),
            P(("pipe", "expert"), None),
            P("pipe", None, "expert"),
            P("pipe", None, "expert"),
            P("pipe", "expert", None),
        ),
        check_vma=False,
    )
```

```python
import jax
import jax.numpy as jnp
from jax import lax
from jax.experimental import pallas as pl
from jax.experimental.pallas import tpu as pltpu
from jax.sharding import PartitionSpec as P

CAP = 8
NY = 4
NX = 4
STAGES = 4
WIDE = 896
NARROW = 256
MESH = pl.DeviceIdType.MESH
F32 = jnp.float32
BF16 = jnp.bfloat16


def dot(a, b):
    return jnp.dot(a, b, preferred_element_type=F32)


def loop(n, body):
    def step(i, carry):
        body(i)
        return carry

    lax.fori_loop(0, n, step, 0)


def span(start, size):
    return pl.ds(pl.multiple_of(start, 128), size)


def route(ids, gates):
    count = ids.shape[1]
    hits, chosen = [], []
    for expert in range(NY):
        match = ids == expert
        hits.append(jnp.sum(match.astype(F32), axis=0, keepdims=True))
        chosen.append(jnp.sum(jnp.where(match, gates, 0.0), axis=0, keepdims=True))
    tri = lax.broadcasted_iota(jnp.int32, (count, count), 0) <= lax.broadcasted_iota(jnp.int32, (count, count), 1)
    stacked = jnp.concatenate([jnp.broadcast_to(hit, (CAP, count)) for hit in hits], axis=0)
    slots = dot(stacked.astype(BF16), tri.astype(F32).astype(BF16)) - 1.0
    level = lax.rem(lax.broadcasted_iota(jnp.int32, (NY * CAP, count), 0), CAP).astype(F32)
    place = jnp.where(slots == level, stacked, 0.0)
    gate = jnp.concatenate([jnp.broadcast_to(row, (CAP, count)) for row in chosen], axis=0)
    return place, jnp.sum(place * gate, axis=1, keepdims=True)


def kernel(
    tok_hbm, cot_hbm, ids_hbm, gates_hbm, wg_hbm, wu_hbm, wd_hbm,
    fb, gg_hbm, gu_hbm, gd_hbm,
    tok, cot, ids, gates, place, gsl, wcat, wcatT, wd, wdT, sb, xs, x2d, s2d, part, own_send, own_recv,
    pair_send, pair_recv, hb, h16, dgu16, ob, rb, gg, gu, gd,
    in_sem, wsend, wrecv, zsend, recv, fsend, asend, arecv, bsend, brecv, hsend, hrecv,
    rsend, rrecv, osend, orecv, gsend, grecv, gown,
):
    quarter = wd.shape[1]
    p = lax.axis_index("pipe")
    e = lax.axis_index("expert")
    y = lax.div(e, 8)
    zh = lax.rem(lax.div(e, 4), 2)
    x = lax.rem(e, 4)
    yz = e - x
    h = lax.div(p, 4)
    q = p + h * (7 - 2 * p)
    shift = lax.rem(q, 2)
    u = lax.rem(x + 3 * shift, 4)
    role = lax.div(lax.rem(u + 1, 4), 2)
    other = 1 - role
    partner = lax.rem(u + 1 - 2 * lax.rem(u, 2) + shift, 4)
    twin = lax.rem(3 - u + shift, 4)
    across = lax.rem(x + 2, 4)
    inner = lax.div(lax.rem(lax.div(p, 2) + 1, 4), 2)
    gid = h * 2 + zh

    def rank_of(hh):
        return q + hh * (7 - 2 * q)

    def place_of(d):
        hh = lax.rem(h + lax.div(d, 2), 2)
        zz = lax.rem(zh + lax.rem(d, 2), 2)
        return hh, zz

    nearest = (0, 3 - inner, 2 + inner, 1)

    def remote(src, dst, ssem, rsem, rank, expert):
        return pltpu.make_async_remote_copy(
            src_ref=src, dst_ref=dst, send_sem=ssem, recv_sem=rsem,
            device_id=(rank, expert), device_id_type=MESH)

    def arrived(ref, sem):
        pltpu.make_async_copy(ref, ref, sem).wait()

    barrier = pltpu.get_barrier_semaphore()

    def greet(t):
        j, d, side = lax.div(t, 8), lax.rem(lax.div(t, 2), 4), lax.rem(t, 2)
        hh, zz = place_of(d)
        xx = x + side * (partner - x)
        pl.semaphore_signal(
            barrier, inc=1, device_id=(rank_of(hh), lax.rem(y + j, 4) * 8 + zz * 4 + xx), device_id_type=MESH)

    loop(31, lambda t: greet(t + 1))
    pl.semaphore_signal(barrier, inc=1, device_id=(p, yz + twin), device_id_type=MESH)

    mine, theirs = span(role * quarter, quarter), span(other * quarter, quarter)
    gate_cols, up_cols, down_rows = span(role * 256, 128), span(role * 256 + 128, 128), span(role * 128, 128)
    loads = [
        pltpu.make_async_copy(ids_hbm, ids, in_sem.at[0]),
        pltpu.make_async_copy(gates_hbm, gates, in_sem.at[1]),
        pltpu.make_async_copy(tok_hbm, tok, in_sem.at[2]),
        pltpu.make_async_copy(cot_hbm, cot, in_sem.at[3]),
        pltpu.make_async_copy(wg_hbm.at[mine, :], wcat.at[:, gate_cols], in_sem.at[4]),
        pltpu.make_async_copy(wu_hbm.at[mine, :], wcat.at[:, up_cols], in_sem.at[5]),
        pltpu.make_async_copy(wd_hbm.at[:, mine], wd.at[down_rows, :], in_sem.at[6]),
    ]
    weights = [
        remote(wg_hbm.at[theirs, :], wcat.at[:, gate_cols], wsend.at[0], wrecv.at[0], p, yz + partner),
        remote(wu_hbm.at[theirs, :], wcat.at[:, up_cols], wsend.at[1], wrecv.at[1], p, yz + partner),
        remote(wd_hbm.at[:, theirs], wd.at[down_rows, :], wsend.at[2], wrecv.at[2], p, yz + partner),
    ]
    for load in loads:
        load.start()
    for load in loads[:2]:
        load.wait()
    placed, gate_slot = route(ids[...], gates[...])
    place[...] = placed.astype(BF16)
    gsl[...] = gate_slot
    for load in loads[2:4]:
        load.wait()

    def slot_rows(ct):
        k, col = lax.div(ct, 2), lax.rem(ct, 2)
        hf, ro = lax.div(k, 2), lax.rem(k, 2)
        cols, to = span(ct * WIDE, WIDE), span(col * WIDE, WIDE)
        rows = dot(place[...], tok[:, cols])
        sb[:, hf, ro, 0, :, to] = rows.reshape(NY, CAP, WIDE).astype(BF16)
        raw = dot(place[...], cot[:, cols]) * gsl[...]
        sb[:, hf, ro, 1, :, to] = raw.reshape(NY, CAP, WIDE).astype(BF16)

    loop(8, slot_rows)
    pl.semaphore_wait(barrier, 32)

    own_s = y * 4 + gid
    local = pltpu.make_async_copy(sb.at[y, h, role], xs.at[x, own_s], recv.at[x, own_s])

    def zcopy(i, d, side):
        hh, zz = place_of(d)
        yy = lax.rem(y + 4 - i, 4)
        ro = role + side * (1 - 2 * role)
        xx = partner if side else x
        return remote(sb.at[yy, hh, ro], xs.at[x, own_s], zsend.at[i, d, side], recv.at[x, own_s],
                      rank_of(hh), yy * 8 + zz * 4 + xx)

    def send_out(i):
        for d in nearest[:0:-1]:
            zcopy(i, d, 0).start()
            zcopy(i, d, 1).start()
        zcopy(i, 0, 1).start()

        @pl.when(i == 0)
        def _():
            local.start()

        @pl.when(i > 0)
        def _():
            zcopy(i, 0, 0).start()

    def base(i):
        return lax.rem(y + i, 4) * 4

    def source(i, d):
        hh, zz = place_of(d)
        return base(i) + hh * 2 + zz

    def fcopy(s, side):
        c = partner if side else x
        return remote(xs.at[c, s], xs.at[c, s], fsend.at[side, s], recv.at[c, s], p, yz + twin)

    def forward(i):
        for d in nearest:
            s = source(i, d)
            for side, c in ((0, x), (1, partner)):
                arrived(xs.at[c, s], recv.at[c, s])
                fcopy(s, side).start()

    def rows_of(i):
        return span(i * 128, 128)

    def acopy(i):
        return remote(own_send.at[i], own_recv.at[i], asend.at[i], arecv.at[i], p, yz + partner)

    def bcopy(i):
        return remote(pair_send.at[i], pair_recv.at[i], bsend.at[i], brecv.at[i], 7 - p, e)

    def hcopy(i):
        return remote(hb.at[i, role], hb.at[i, role], hsend.at[i], hrecv.at[i], p, yz + partner)

    def first_dots(i):
        def rest(j):
            s = base(i) + j
            arrived(xs.at[twin, s], recv.at[twin, s])
            arrived(xs.at[across, s], recv.at[across, s])

        loop(4, rest)

        def flatten(c):
            to = pl.ds(pl.multiple_of(i * 128 + c * 32, 32), 32)
            x2d[to, :] = xs[c, pl.ds(base(i), 4), 0].astype(F32).reshape(32, quarter).astype(BF16)
            s2d[to, :] = xs[c, pl.ds(base(i), 4), 1].astype(F32).reshape(32, quarter).astype(BF16)

        loop(4, flatten)
        rows = rows_of(i)
        pre = dot(x2d[rows, :], wcat[...])
        dh = dot(s2d[rows, :], wdT[...])
        for k in range(2):
            part[i, k, :, 0:256] = pre[:, k * 256:k * 256 + 256]
            part[i, k, :, 256:384] = dh[:, k * 128:k * 128 + 128]
        own_send[i] = part[i, other].reshape(16, 8, 384).astype(BF16)
        acopy(i).start()

    def add_partner(i):
        arrived(own_recv.at[i], arecv.at[i])
        both = part[i, role] + own_recv[i].astype(F32).reshape(128, 384)
        part[i, role] = both
        pair_send[i] = both.reshape(16, 8, 384).astype(BF16)
        bcopy(i).start()

    def activate(i):
        arrived(pair_recv.at[i], brecv.at[i])
        whole = part[i, role] + pair_recv[i].astype(F32).reshape(128, 384)
        gate, up, dh = whole[:, 0:128], whole[:, 128:256], whole[:, 256:384]
        sigma = jax.nn.sigmoid(gate)
        active = gate * sigma
        hb[i, role, :, :, 0:128] = (active * up).reshape(16, 8, 128).astype(BF16)
        dgate = dh * up * sigma * (1.0 + gate * (1.0 - sigma))
        hb[i, role, :, :, 128:256] = dgate.reshape(16, 8, 128).astype(BF16)
        hb[i, role, :, :, 256:384] = (dh * active).reshape(16, 8, 128).astype(BF16)
        hcopy(i).start()

    def rcopy(s, side):
        c = across if side else twin
        return remote(ob.at[c, s], rb.at[side, s], rsend.at[side, s], rrecv.at[side, s], p, yz + twin)

    def second_dots(i):
        rows = rows_of(i)
        arrived(hb.at[i, other], hrecv.at[i])
        for k in range(2):
            flat = hb[i, k].astype(F32).reshape(128, 384).astype(BF16)
            h16[rows, k * 128:k * 128 + 128] = flat[:, 0:128]
            dgu16[rows, k * 256:k * 256 + 256] = flat[:, 128:384]

        def tile(ct):
            cols = span(ct * WIDE, WIDE)
            out = dot(h16[rows, :], wd[:, cols])
            ob[:, pl.ds(base(i), 4), 0, :, cols] = out.reshape(NX, 4, CAP, WIDE).astype(BF16)
            back = dot(dgu16[rows, :], wcatT[:, cols])
            ob[:, pl.ds(base(i), 4), 1, :, cols] = back.reshape(NX, 4, CAP, WIDE).astype(BF16)

        loop(2, tile)
        for d in nearest[::-1]:
            s = source(i, d)
            rcopy(s, 0).start()
            rcopy(s, 1).start()

    def seat(hf, ro, zz):
        return (hf * 2 + ro) * 2 + zz

    def ocopy(i, d, side):
        hh, zz = place_of(d)
        yy = lax.rem(y + i, 4)
        s = source(i, d)
        c = partner if side else x
        return remote(ob.at[c, s], fb.at[y, seat(h, role, zh)], osend.at[side, s], orecv.at[y, seat(h, role, zh)],
                      rank_of(hh), yy * 8 + zz * 4 + c)

    own_out = pltpu.make_async_copy(ob.at[x, own_s], fb.at[y, seat(h, role, zh)], orecv.at[y, seat(h, role, zh)])

    def add_twin(i):
        for d in nearest[::-1]:
            s = source(i, d)
            for side, c in ((0, x), (1, partner)):
                arrived(rb.at[side, s], rrecv.at[side, s])
                ob[c, s] = (ob[c, s].astype(F32) + rb[side, s].astype(F32)).astype(BF16)
                if side == 1 or d is not nearest[0]:
                    ocopy(i, d, side).start()
                    continue

                @pl.when(i == 0)
                def _():
                    own_out.start()

                @pl.when(i > 0)
                def _():
                    ocopy(i, d, side).start()

    def weight_grads(k):
        dguT = dgu16[:, span(k * 256, 256)].T
        hT = h16[:, span(k * 128, 128)].T

        def tile(ct):
            cols = span(ct * NARROW, NARROW)
            both = dot(dguT, x2d[:, cols]).T
            gg[k, cols, :] = both[:, 0:128].astype(BF16)
            gu[k, cols, :] = both[:, 128:256].astype(BF16)
            gd[k, :, cols] = dot(hT, s2d[:, cols]).astype(BF16)

        loop(quarter // NARROW, tile)

    grads_away = [
        remote(gg.at[other], gg_hbm.at[mine, :], gsend.at[0], grecv.at[0], p, yz + partner),
        remote(gu.at[other], gu_hbm.at[mine, :], gsend.at[1], grecv.at[1], p, yz + partner),
        remote(gd.at[other], gd_hbm.at[:, mine], gsend.at[2], grecv.at[2], p, yz + partner),
    ]
    grads_own = [
        pltpu.make_async_copy(gg.at[role], gg_hbm.at[mine, :], gown.at[0]),
        pltpu.make_async_copy(gu.at[role], gu_hbm.at[mine, :], gown.at[1]),
        pltpu.make_async_copy(gd.at[role], gd_hbm.at[:, mine], gown.at[2]),
    ]

    send_out(0)
    for copy in weights:
        copy.start()
    forward(0)
    send_out(1)
    for load in loads[4:]:
        load.wait()
    for copy in weights:
        copy.wait_recv()

    def turn(ct):
        cols = span(ct * NARROW, NARROW)
        wcatT[:, cols] = wcat[cols, :].T
        wdT[cols, :] = wd[:, cols].T

    loop(quarter // NARROW, turn)

    def turn_of(i):
        @pl.when(i < 4)
        def _():
            first_dots(i)

        @pl.when(jnp.logical_and(i >= 1, i < 5))
        def _():
            activate(i - 1)

        @pl.when(i < 3)
        def _():
            forward(i + 1)

        @pl.when(i < 2)
        def _():
            send_out(i + 2)

        @pl.when(i < 4)
        def _():
            add_partner(i)

        @pl.when(jnp.logical_and(i >= 1, i < 5))
        def _():
            second_dots(i - 1)

        @pl.when(i == 4)
        def _():
            weight_grads(other)
            for copy in grads_away:
                copy.start()

        @pl.when(i >= 2)
        def _():
            add_twin(i - 2)

    loop(6, turn_of)
    weight_grads(role)
    for copy in grads_own:
        copy.start()

    for copy in weights + grads_away:
        copy.wait_send()
    for i in range(STAGES):
        for side in range(2):
            for d in range(4):
                if (i, d, side) != (0, 0, 0):
                    zcopy(i, d, side).wait_send()

    def sent(i):
        for d in range(4):
            s = source(i, d)
            for side in range(2):
                fcopy(s, side).wait_send()
                rcopy(s, side).wait_send()
                if side == 1 or d > 0:
                    ocopy(i, d, side).wait_send()

        @pl.when(i > 0)
        def _():
            ocopy(i, 0, 0).wait_send()

        acopy(i).wait_send()
        bcopy(i).wait_send()
        hcopy(i).wait_send()

    loop(STAGES, sent)

    def landed(t):
        k, n = lax.div(t, 8), lax.rem(t, 8)
        arrived(fb.at[k, n], orecv.at[k, n])

    loop(32, landed)
    for copy in grads_own:
        copy.wait()
    for copy in grads_away:
        copy.wait_recv()


def finish(
    ids_ref, gates_ref, fb_hbm, gg_in, gu_in, gd_in, mixed_hbm, igrad_hbm, gg_out, gu_out, gd_out,
    fb, mixed, igrad, gg, gu, gd, in_sem, out_sem, pass_sem,
):
    quarter = fb.shape[-1]
    grads = ((gg_in, gg, gg_out), (gu_in, gu, gu_out), (gd_in, gd, gd_out))
    enter = [pltpu.make_async_copy(grad[0], grad[1], pass_sem.at[0, n]) for n, grad in enumerate(grads)]
    leave = [pltpu.make_async_copy(grad[1], grad[2], pass_sem.at[1, n]) for n, grad in enumerate(grads)]
    fetch = [
        pltpu.make_async_copy(fb_hbm.at[:, pl.ds(2 * n, 2)], fb.at[:, pl.ds(2 * n, 2)], in_sem.at[n]) for n in range(4)
    ]
    for copy in fetch + enter:
        copy.start()
    place, gsl = route(ids_ref[...], gates_ref[...])
    placeT = place.T.astype(BF16)
    stores = []
    for n in range(4):
        fetch[n].wait()
        for col in range(0, quarter, WIDE):
            fr, to = pl.ds(col, WIDE), pl.ds(n * quarter + col, WIDE)

            def both(k):
                return (fb[:, 2 * n, k, :, fr].astype(F32) + fb[:, 2 * n + 1, k, :, fr].astype(F32)).reshape(32, WIDE)

            mixed[:, to] = dot(placeT, (both(0) * gsl).astype(BF16)).astype(BF16)
            igrad[:, to] = dot(placeT, both(1).astype(BF16)).astype(BF16)
        if n == 0:
            for get, put in zip(enter, leave):
                get.wait()
                put.start()
        cols = pl.ds(n * quarter, quarter)
        stores += [
            pltpu.make_async_copy(mixed.at[:, cols], mixed_hbm.at[:, cols], out_sem.at[n, 0]),
            pltpu.make_async_copy(igrad.at[:, cols], igrad_hbm.at[:, cols], out_sem.at[n, 1]),
        ]
        stores[-2].start()
        stores[-1].start()
    for copy in stores + leave:
        copy.wait()


def per_device(tokens, cotangent, expert_ids, gate_weights, w_gate, w_up, w_down):
    tok_count, width = tokens.shape
    half, quarter = width // 2, width // 4
    ids, gates = expert_ids.T, gate_weights.T
    dma = pltpu.SemaphoreType.DMA
    vmem = pltpu.VMEM
    piece = (2, CAP, quarter)
    swap = (STAGES, 16, 8, 384)
    any_spec = pl.BlockSpec(memory_space=pl.ANY)
    outs = pl.pallas_call(
        kernel,
        out_shape=(
            jax.ShapeDtypeStruct((NY, 8) + piece, BF16),
            jax.ShapeDtypeStruct((half, 128), BF16),
            jax.ShapeDtypeStruct((half, 128), BF16),
            jax.ShapeDtypeStruct((128, half), BF16),
        ),
        in_specs=[any_spec] * 7,
        out_specs=[any_spec] * 4,
        scratch_shapes=[
            vmem((tok_count, width), BF16),
            vmem((tok_count, width), BF16),
            vmem(ids.shape, jnp.int32),
            vmem(gates.shape, F32),
            vmem((32, tok_count), BF16),
            vmem((32, 1), F32),
            vmem((quarter, 512), BF16),
            vmem((512, quarter), BF16),
            vmem((256, quarter), BF16),
            vmem((quarter, 256), BF16),
            vmem((NY, 2, 2) + piece, BF16),
            vmem((NX, 16) + piece, BF16),
            vmem((512, quarter), BF16),
            vmem((512, quarter), BF16),
            vmem((STAGES, 2, 128, 384), F32),
            vmem(swap, BF16),
            vmem(swap, BF16),
            vmem(swap, BF16),
            vmem(swap, BF16),
            vmem((STAGES, 2, 16, 8, 384), BF16),
            vmem((512, 256), BF16),
            vmem((512, 512), BF16),
            vmem((NX, 16) + piece, BF16),
            vmem((2, 16) + piece, BF16),
            vmem((2, quarter, 128), BF16),
            vmem((2, quarter, 128), BF16),
            vmem((2, 128, quarter), BF16),
            dma((7,)),
            dma((3,)),
            dma((3,)),
            dma((STAGES, 4, 2)),
            dma((NX, 16)),
            dma((2, 16)),
            dma((STAGES,)),
            dma((STAGES,)),
            dma((STAGES,)),
            dma((STAGES,)),
            dma((STAGES,)),
            dma((STAGES,)),
            dma((2, 16)),
            dma((2, 16)),
            dma((2, 16)),
            dma((NY, 8)),
            dma((3,)),
            dma((3,)),
            dma((3,)),
        ],
        compiler_params=pltpu.CompilerParams(
            collective_id=0, has_side_effects=True, vmem_limit_bytes=56 * 1024 * 1024
        ),
    )(tokens, cotangent, ids, gates, w_gate[0], w_up[0], w_down[0])
    whole = pl.BlockSpec(memory_space=vmem)
    mixed, igrad, gg, gu, gd = pl.pallas_call(
        finish,
        out_shape=(
            jax.ShapeDtypeStruct((tok_count, width), BF16),
            jax.ShapeDtypeStruct((tok_count, width), BF16),
            jax.ShapeDtypeStruct((half, 128), BF16),
            jax.ShapeDtypeStruct((half, 128), BF16),
            jax.ShapeDtypeStruct((128, half), BF16),
        ),
        in_specs=[whole] * 2 + [any_spec] * 4,
        out_specs=[any_spec] * 5,
        scratch_shapes=[
            vmem((NY, 8) + piece, BF16),
            vmem((tok_count, width), BF16),
            vmem((tok_count, width), BF16),
            vmem((half, 128), BF16),
            vmem((half, 128), BF16),
            vmem((128, half), BF16),
            dma((4,)),
            dma((4, 2)),
            dma((2, 3)),
        ],
        compiler_params=pltpu.CompilerParams(vmem_limit_bytes=56 * 1024 * 1024),
    )(ids, gates, *outs)
    return mixed, igrad, gg[None], gu[None], gd[None]


def solution(mesh):
    return jax.shard_map(
        per_device,
        mesh=mesh,
        in_specs=(
            P(("pipe", "expert"), None),
            P(("pipe", "expert"), None),
            P(("pipe", "expert"), None),
            P(("pipe", "expert"), None),
            P("pipe", None, "expert"),
            P("pipe", None, "expert"),
            P("pipe", "expert", None),
        ),
        out_specs=(
            P(("pipe", "expert"), None),
            P(("pipe", "expert"), None),
            P("pipe", None, "expert"),
            P("pipe", None, "expert"),
            P("pipe", "expert", None),
        ),
        check_vma=False,
    )
```

```python
import jax
import jax.numpy as jnp
from jax import lax
from jax.experimental import pallas as pl
from jax.experimental.pallas import tpu as pltpu
from jax.sharding import PartitionSpec as P

CAP = 8
NY = 4
NX = 4
STAGES = 4
WIDE = 896
NARROW = 256
MESH = pl.DeviceIdType.MESH
F32 = jnp.float32
BF16 = jnp.bfloat16


def dot(a, b):
    return jnp.dot(a, b, preferred_element_type=F32)


def loop(n, body):
    def step(i, carry):
        body(i)
        return carry

    lax.fori_loop(0, n, step, 0)


def span(start, size):
    return pl.ds(pl.multiple_of(start, 128), size)


def route(ids, gates):
    count = ids.shape[1]
    hits, chosen = [], []
    for expert in range(NY):
        match = ids == expert
        hits.append(jnp.sum(match.astype(F32), axis=0, keepdims=True))
        chosen.append(jnp.sum(jnp.where(match, gates, 0.0), axis=0, keepdims=True))
    tri = lax.broadcasted_iota(jnp.int32, (count, count), 0) <= lax.broadcasted_iota(jnp.int32, (count, count), 1)
    stacked = jnp.concatenate([jnp.broadcast_to(hit, (CAP, count)) for hit in hits], axis=0)
    slots = dot(stacked.astype(BF16), tri.astype(F32).astype(BF16)) - 1.0
    level = lax.rem(lax.broadcasted_iota(jnp.int32, (NY * CAP, count), 0), CAP).astype(F32)
    place = jnp.where(slots == level, stacked, 0.0)
    gate = jnp.concatenate([jnp.broadcast_to(row, (CAP, count)) for row in chosen], axis=0)
    return place, jnp.sum(place * gate, axis=1, keepdims=True)


def kernel(
    tok_hbm, cot_hbm, ids_hbm, gates_hbm, wg_hbm, wu_hbm, wd_hbm,
    fb, gg_hbm, gu_hbm, gd_hbm,
    tok, cot, ids, gates, place, gsl, wcat, wcatT, wd, wdT, sb, xs, x2d, s2d, part, own_send, own_recv,
    pair_send, pair_recv, hb, h16, dgu16, ob, rb, gg, gu, gd,
    in_sem, wsend, wrecv, zsend, recv, fsend, asend, arecv, bsend, brecv, hsend, hrecv,
    rsend, rrecv, osend, orecv, gsend, grecv, gown,
):
    quarter = wd.shape[1]
    p = lax.axis_index("pipe")
    e = lax.axis_index("expert")
    y = lax.div(e, 8)
    zh = lax.rem(lax.div(e, 4), 2)
    x = lax.rem(e, 4)
    yz = e - x
    h = lax.div(p, 4)
    q = p + h * (7 - 2 * p)
    shift = lax.rem(q, 2)
    u = lax.rem(x + 3 * shift, 4)
    role = lax.div(lax.rem(u + 1, 4), 2)
    other = 1 - role
    partner = lax.rem(u + 1 - 2 * lax.rem(u, 2) + shift, 4)
    twin = lax.rem(3 - u + shift, 4)
    across = lax.rem(x + 2, 4)
    inner = lax.div(lax.rem(lax.div(p, 2) + 1, 4), 2)
    gid = h * 2 + zh

    def rank_of(hh):
        return q + hh * (7 - 2 * q)

    def place_of(d):
        hh = lax.rem(h + lax.div(d, 2), 2)
        zz = lax.rem(zh + lax.rem(d, 2), 2)
        return hh, zz

    nearest = (0, 3 - inner, 2 + inner, 1)

    def remote(src, dst, ssem, rsem, rank, expert):
        return pltpu.make_async_remote_copy(
            src_ref=src, dst_ref=dst, send_sem=ssem, recv_sem=rsem,
            device_id=(rank, expert), device_id_type=MESH)

    def arrived(ref, sem):
        pltpu.make_async_copy(ref, ref, sem).wait()

    barrier = pltpu.get_barrier_semaphore()

    def greet(t):
        j, d, side = lax.div(t, 8), lax.rem(lax.div(t, 2), 4), lax.rem(t, 2)
        hh, zz = place_of(d)
        xx = x + side * (partner - x)
        pl.semaphore_signal(
            barrier, inc=1, device_id=(rank_of(hh), lax.rem(y + j, 4) * 8 + zz * 4 + xx), device_id_type=MESH)

    loop(31, lambda t: greet(t + 1))
    pl.semaphore_signal(barrier, inc=1, device_id=(p, yz + twin), device_id_type=MESH)

    mine, theirs = span(role * quarter, quarter), span(other * quarter, quarter)
    gate_cols, up_cols, down_rows = span(role * 256, 128), span(role * 256 + 128, 128), span(role * 128, 128)
    loads = [
        pltpu.make_async_copy(ids_hbm, ids, in_sem.at[0]),
        pltpu.make_async_copy(gates_hbm, gates, in_sem.at[1]),
        pltpu.make_async_copy(tok_hbm, tok, in_sem.at[2]),
        pltpu.make_async_copy(cot_hbm, cot, in_sem.at[3]),
        pltpu.make_async_copy(wg_hbm.at[mine, :], wcat.at[:, gate_cols], in_sem.at[4]),
        pltpu.make_async_copy(wu_hbm.at[mine, :], wcat.at[:, up_cols], in_sem.at[5]),
        pltpu.make_async_copy(wd_hbm.at[:, mine], wd.at[down_rows, :], in_sem.at[6]),
    ]
    weights = [
        remote(wg_hbm.at[theirs, :], wcat.at[:, gate_cols], wsend.at[0], wrecv.at[0], p, yz + partner),
        remote(wu_hbm.at[theirs, :], wcat.at[:, up_cols], wsend.at[1], wrecv.at[1], p, yz + partner),
        remote(wd_hbm.at[:, theirs], wd.at[down_rows, :], wsend.at[2], wrecv.at[2], p, yz + partner),
    ]
    for load in loads:
        load.start()
    for load in loads[:2]:
        load.wait()
    placed, gate_slot = route(ids[...], gates[...])
    place[...] = placed.astype(BF16)
    gsl[...] = gate_slot
    for load in loads[2:4]:
        load.wait()

    def slot_rows(ct):
        k, col = lax.div(ct, 2), lax.rem(ct, 2)
        hf, ro = lax.div(k, 2), lax.rem(k, 2)
        cols, to = span(ct * WIDE, WIDE), span(col * WIDE, WIDE)
        rows = dot(place[...], tok[:, cols])
        sb[:, hf, ro, 0, :, to] = rows.reshape(NY, CAP, WIDE).astype(BF16)
        raw = dot(place[...], cot[:, cols]) * gsl[...]
        sb[:, hf, ro, 1, :, to] = raw.reshape(NY, CAP, WIDE).astype(BF16)

    loop(8, slot_rows)
    pl.semaphore_wait(barrier, 32)

    own_s = y * 4 + gid
    local = pltpu.make_async_copy(sb.at[y, h, role], xs.at[x, own_s], recv.at[x, own_s])

    def zcopy(i, d, side):
        hh, zz = place_of(d)
        yy = lax.rem(y + 4 - i, 4)
        ro = role + side * (1 - 2 * role)
        xx = partner if side else x
        return remote(sb.at[yy, hh, ro], xs.at[x, own_s], zsend.at[i, d, side], recv.at[x, own_s],
                      rank_of(hh), yy * 8 + zz * 4 + xx)

    def send_far(i):
        for d in nearest[:0:-1]:
            zcopy(i, d, 1).start()
        zcopy(i, 0, 1).start()

    def send_out(i):
        send_near(i)
        send_far(i)

    def send_near(i):
        for d in nearest[:0:-1]:
            zcopy(i, d, 0).start()

        @pl.when(i == 0)
        def _():
            local.start()

        @pl.when(i > 0)
        def _():
            zcopy(i, 0, 0).start()

    def base(i):
        return lax.rem(y + i, 4) * 4

    def source(i, d):
        hh, zz = place_of(d)
        return base(i) + hh * 2 + zz

    def fcopy(s, side):
        c = partner if side else x
        return remote(xs.at[c, s], xs.at[c, s], fsend.at[side, s], recv.at[c, s], p, yz + twin)

    def forward(i):
        for d in nearest:
            s = source(i, d)
            for side, c in ((0, x), (1, partner)):
                arrived(xs.at[c, s], recv.at[c, s])
                fcopy(s, side).start()

    def rows_of(i):
        return span(i * 128, 128)

    def acopy(i):
        return remote(own_send.at[i], own_recv.at[i], asend.at[i], arecv.at[i], p, yz + partner)

    def bcopy(i):
        return remote(pair_send.at[i], pair_recv.at[i], bsend.at[i], brecv.at[i], 7 - p, e)

    def hcopy(i):
        return remote(hb.at[i, role], hb.at[i, role], hsend.at[i], hrecv.at[i], p, yz + partner)

    def first_dots(i):
        def rest(j):
            s = base(i) + j
            arrived(xs.at[twin, s], recv.at[twin, s])
            arrived(xs.at[across, s], recv.at[across, s])

        loop(4, rest)

        def flatten(c):
            to = pl.ds(pl.multiple_of(i * 128 + c * 32, 32), 32)
            x2d[to, :] = xs[c, pl.ds(base(i), 4), 0].astype(F32).reshape(32, quarter).astype(BF16)
            s2d[to, :] = xs[c, pl.ds(base(i), 4), 1].astype(F32).reshape(32, quarter).astype(BF16)

        loop(4, flatten)
        rows = rows_of(i)
        pre = dot(x2d[rows, :], wcat[...])
        dh = dot(s2d[rows, :], wdT[...])
        for k in range(2):
            part[i, k, :, 0:256] = pre[:, k * 256:k * 256 + 256]
            part[i, k, :, 256:384] = dh[:, k * 128:k * 128 + 128]
        own_send[i] = part[i, other].reshape(16, 8, 384).astype(BF16)
        acopy(i).start()

    def add_partner(i):
        arrived(own_recv.at[i], arecv.at[i])
        both = part[i, role] + own_recv[i].astype(F32).reshape(128, 384)
        part[i, role] = both
        pair_send[i] = both.reshape(16, 8, 384).astype(BF16)
        bcopy(i).start()

    def activate(i):
        arrived(pair_recv.at[i], brecv.at[i])
        whole = part[i, role] + pair_recv[i].astype(F32).reshape(128, 384)
        gate, up, dh = whole[:, 0:128], whole[:, 128:256], whole[:, 256:384]
        sigma = jax.nn.sigmoid(gate)
        active = gate * sigma
        hb[i, role, :, :, 0:128] = (active * up).reshape(16, 8, 128).astype(BF16)
        dgate = dh * up * sigma * (1.0 + gate * (1.0 - sigma))
        hb[i, role, :, :, 128:256] = dgate.reshape(16, 8, 128).astype(BF16)
        hb[i, role, :, :, 256:384] = (dh * active).reshape(16, 8, 128).astype(BF16)
        hcopy(i).start()

    def rcopy(s, side):
        c = across if side else twin
        return remote(ob.at[c, s], rb.at[side, s], rsend.at[side, s], rrecv.at[side, s], p, yz + twin)

    def second_dots(i):
        rows = rows_of(i)
        arrived(hb.at[i, other], hrecv.at[i])
        for k in range(2):
            flat = hb[i, k].astype(F32).reshape(128, 384).astype(BF16)
            h16[rows, k * 128:k * 128 + 128] = flat[:, 0:128]
            dgu16[rows, k * 256:k * 256 + 256] = flat[:, 128:384]

        def tile(ct):
            cols = span(ct * WIDE, WIDE)
            out = dot(h16[rows, :], wd[:, cols])
            ob[:, pl.ds(base(i), 4), 0, :, cols] = out.reshape(NX, 4, CAP, WIDE).astype(BF16)
            back = dot(dgu16[rows, :], wcatT[:, cols])
            ob[:, pl.ds(base(i), 4), 1, :, cols] = back.reshape(NX, 4, CAP, WIDE).astype(BF16)

        loop(2, tile)
        for d in nearest[::-1]:
            s = source(i, d)
            rcopy(s, 0).start()
            rcopy(s, 1).start()

    def seat(hf, ro, zz):
        return (hf * 2 + ro) * 2 + zz

    def ocopy(i, d, side):
        hh, zz = place_of(d)
        yy = lax.rem(y + i, 4)
        s = source(i, d)
        c = partner if side else x
        return remote(ob.at[c, s], fb.at[y, seat(h, role, zh)], osend.at[side, s], orecv.at[y, seat(h, role, zh)],
                      rank_of(hh), yy * 8 + zz * 4 + c)

    own_out = pltpu.make_async_copy(ob.at[x, own_s], fb.at[y, seat(h, role, zh)], orecv.at[y, seat(h, role, zh)])

    def add_twin(i, side):
        c = partner if side else x
        for d in nearest[::-1]:
            s = source(i, d)
            arrived(rb.at[side, s], rrecv.at[side, s])
            ob[c, s] = (ob[c, s].astype(F32) + rb[side, s].astype(F32)).astype(BF16)
            if side == 1 or d is not nearest[0]:
                ocopy(i, d, side).start()
                continue

            @pl.when(i == 0)
            def _():
                own_out.start()

            @pl.when(i > 0)
            def _():
                ocopy(i, d, side).start()

    def weight_grads(k):
        dguT = dgu16[:, span(k * 256, 256)].T
        hT = h16[:, span(k * 128, 128)].T

        def tile(ct):
            cols = span(ct * NARROW, NARROW)
            both = dot(dguT, x2d[:, cols]).T
            gg[k, cols, :] = both[:, 0:128].astype(BF16)
            gu[k, cols, :] = both[:, 128:256].astype(BF16)
            gd[k, :, cols] = dot(hT, s2d[:, cols]).astype(BF16)

        loop(quarter // NARROW, tile)

    grads_away = [
        remote(gg.at[other], gg_hbm.at[mine, :], gsend.at[0], grecv.at[0], p, yz + partner),
        remote(gu.at[other], gu_hbm.at[mine, :], gsend.at[1], grecv.at[1], p, yz + partner),
        remote(gd.at[other], gd_hbm.at[:, mine], gsend.at[2], grecv.at[2], p, yz + partner),
    ]
    grads_own = [
        pltpu.make_async_copy(gg.at[role], gg_hbm.at[mine, :], gown.at[0]),
        pltpu.make_async_copy(gu.at[role], gu_hbm.at[mine, :], gown.at[1]),
        pltpu.make_async_copy(gd.at[role], gd_hbm.at[:, mine], gown.at[2]),
    ]

    send_out(0)
    send_out(1)
    send_out(2)
    send_out(3)
    for copy in weights:
        copy.start()
    forward(0)
    for load in loads[4:]:
        load.wait()
    for copy in weights:
        copy.wait_recv()

    def turn(ct):
        cols = span(ct * NARROW, NARROW)
        wcatT[:, cols] = wcat[cols, :].T
        wdT[cols, :] = wd[:, cols].T

    loop(quarter // NARROW, turn)

    def turn_of(i):
        @pl.when(i < 4)
        def _():
            first_dots(i)

        @pl.when(jnp.logical_and(i >= 1, i < 5))
        def _():
            activate(i - 1)

        @pl.when(i < 3)
        def _():
            forward(i + 1)

        @pl.when(i < 4)
        def _():
            add_partner(i)

        @pl.when(jnp.logical_and(i >= 1, i < 5))
        def _():
            second_dots(i - 1)

        @pl.when(i >= 2)
        def _():
            add_twin(i - 2, 0)

        @pl.when(i >= 2)
        def _():
            add_twin(i - 2, 1)

        @pl.when(i == 4)
        def _():
            weight_grads(other)
            for copy in grads_away:
                copy.start()

    loop(6, turn_of)
    weight_grads(role)
    for copy in grads_own:
        copy.start()

    for copy in weights + grads_away:
        copy.wait_send()
    for i in range(STAGES):
        for side in range(2):
            for d in range(4):
                if (i, d, side) != (0, 0, 0):
                    zcopy(i, d, side).wait_send()

    def sent(i):
        for d in range(4):
            s = source(i, d)
            for side in range(2):
                fcopy(s, side).wait_send()
                rcopy(s, side).wait_send()
                if side == 1 or d > 0:
                    ocopy(i, d, side).wait_send()

        @pl.when(i > 0)
        def _():
            ocopy(i, 0, 0).wait_send()

        acopy(i).wait_send()
        bcopy(i).wait_send()
        hcopy(i).wait_send()

    loop(STAGES, sent)

    def landed(t):
        k, n = lax.div(t, 8), lax.rem(t, 8)
        arrived(fb.at[k, n], orecv.at[k, n])

    loop(32, landed)
    for copy in grads_own:
        copy.wait()
    for copy in grads_away:
        copy.wait_recv()


def finish(
    ids_ref, gates_ref, fb_hbm, gg_in, gu_in, gd_in, mixed_hbm, igrad_hbm, gg_out, gu_out, gd_out,
    fb, mixed, igrad, gg, gu, gd, in_sem, out_sem, pass_sem,
):
    quarter = fb.shape[-1]
    grads = ((gg_in, gg, gg_out), (gu_in, gu, gu_out), (gd_in, gd, gd_out))
    enter = [pltpu.make_async_copy(grad[0], grad[1], pass_sem.at[0, n]) for n, grad in enumerate(grads)]
    leave = [pltpu.make_async_copy(grad[1], grad[2], pass_sem.at[1, n]) for n, grad in enumerate(grads)]
    fetch = [
        pltpu.make_async_copy(fb_hbm.at[:, pl.ds(2 * n, 2)], fb.at[:, pl.ds(2 * n, 2)], in_sem.at[n]) for n in range(4)
    ]
    for copy in fetch + enter:
        copy.start()
    place, gsl = route(ids_ref[...], gates_ref[...])
    placeT = place.T.astype(BF16)
    stores = []
    for n in range(4):
        fetch[n].wait()
        for col in range(0, quarter, WIDE):
            fr, to = pl.ds(col, WIDE), pl.ds(n * quarter + col, WIDE)

            def both(k):
                return (fb[:, 2 * n, k, :, fr].astype(F32) + fb[:, 2 * n + 1, k, :, fr].astype(F32)).reshape(32, WIDE)

            mixed[:, to] = dot(placeT, (both(0) * gsl).astype(BF16)).astype(BF16)
            igrad[:, to] = dot(placeT, both(1).astype(BF16)).astype(BF16)
        if n == 0:
            for get, put in zip(enter, leave):
                get.wait()
                put.start()
        cols = pl.ds(n * quarter, quarter)
        stores += [
            pltpu.make_async_copy(mixed.at[:, cols], mixed_hbm.at[:, cols], out_sem.at[n, 0]),
            pltpu.make_async_copy(igrad.at[:, cols], igrad_hbm.at[:, cols], out_sem.at[n, 1]),
        ]
        stores[-2].start()
        stores[-1].start()
    for copy in stores + leave:
        copy.wait()


def per_device(tokens, cotangent, expert_ids, gate_weights, w_gate, w_up, w_down):
    tok_count, width = tokens.shape
    half, quarter = width // 2, width // 4
    ids, gates = expert_ids.T, gate_weights.T
    dma = pltpu.SemaphoreType.DMA
    vmem = pltpu.VMEM
    piece = (2, CAP, quarter)
    swap = (STAGES, 16, 8, 384)
    any_spec = pl.BlockSpec(memory_space=pl.ANY)
    outs = pl.pallas_call(
        kernel,
        out_shape=(
            jax.ShapeDtypeStruct((NY, 8) + piece, BF16),
            jax.ShapeDtypeStruct((half, 128), BF16),
            jax.ShapeDtypeStruct((half, 128), BF16),
            jax.ShapeDtypeStruct((128, half), BF16),
        ),
        in_specs=[any_spec] * 7,
        out_specs=[any_spec] * 4,
        scratch_shapes=[
            vmem((tok_count, width), BF16),
            vmem((tok_count, width), BF16),
            vmem(ids.shape, jnp.int32),
            vmem(gates.shape, F32),
            vmem((32, tok_count), BF16),
            vmem((32, 1), F32),
            vmem((quarter, 512), BF16),
            vmem((512, quarter), BF16),
            vmem((256, quarter), BF16),
            vmem((quarter, 256), BF16),
            vmem((NY, 2, 2) + piece, BF16),
            vmem((NX, 16) + piece, BF16),
            vmem((512, quarter), BF16),
            vmem((512, quarter), BF16),
            vmem((STAGES, 2, 128, 384), F32),
            vmem(swap, BF16),
            vmem(swap, BF16),
            vmem(swap, BF16),
            vmem(swap, BF16),
            vmem((STAGES, 2, 16, 8, 384), BF16),
            vmem((512, 256), BF16),
            vmem((512, 512), BF16),
            vmem((NX, 16) + piece, BF16),
            vmem((2, 16) + piece, BF16),
            vmem((2, quarter, 128), BF16),
            vmem((2, quarter, 128), BF16),
            vmem((2, 128, quarter), BF16),
            dma((7,)),
            dma((3,)),
            dma((3,)),
            dma((STAGES, 4, 2)),
            dma((NX, 16)),
            dma((2, 16)),
            dma((STAGES,)),
            dma((STAGES,)),
            dma((STAGES,)),
            dma((STAGES,)),
            dma((STAGES,)),
            dma((STAGES,)),
            dma((2, 16)),
            dma((2, 16)),
            dma((2, 16)),
            dma((NY, 8)),
            dma((3,)),
            dma((3,)),
            dma((3,)),
        ],
        compiler_params=pltpu.CompilerParams(
            collective_id=0, has_side_effects=True, vmem_limit_bytes=56 * 1024 * 1024
        ),
    )(tokens, cotangent, ids, gates, w_gate[0], w_up[0], w_down[0])
    whole = pl.BlockSpec(memory_space=vmem)
    mixed, igrad, gg, gu, gd = pl.pallas_call(
        finish,
        out_shape=(
            jax.ShapeDtypeStruct((tok_count, width), BF16),
            jax.ShapeDtypeStruct((tok_count, width), BF16),
            jax.ShapeDtypeStruct((half, 128), BF16),
            jax.ShapeDtypeStruct((half, 128), BF16),
            jax.ShapeDtypeStruct((128, half), BF16),
        ),
        in_specs=[whole] * 2 + [any_spec] * 4,
        out_specs=[any_spec] * 5,
        scratch_shapes=[
            vmem((NY, 8) + piece, BF16),
            vmem((tok_count, width), BF16),
            vmem((tok_count, width), BF16),
            vmem((half, 128), BF16),
            vmem((half, 128), BF16),
            vmem((128, half), BF16),
            dma((4,)),
            dma((4, 2)),
            dma((2, 3)),
        ],
        compiler_params=pltpu.CompilerParams(vmem_limit_bytes=56 * 1024 * 1024),
    )(ids, gates, *outs)
    return mixed, igrad, gg[None], gu[None], gd[None]


def solution(mesh):
    return jax.shard_map(
        per_device,
        mesh=mesh,
        in_specs=(
            P(("pipe", "expert"), None),
            P(("pipe", "expert"), None),
            P(("pipe", "expert"), None),
            P(("pipe", "expert"), None),
            P("pipe", None, "expert"),
            P("pipe", None, "expert"),
            P("pipe", "expert", None),
        ),
        out_specs=(
            P(("pipe", "expert"), None),
            P(("pipe", "expert"), None),
            P("pipe", None, "expert"),
            P("pipe", None, "expert"),
            P("pipe", "expert", None),
        ),
        check_vma=False,
    )
```

```python
import jax
import jax.numpy as jnp
from jax import lax
from jax.experimental import pallas as pl
from jax.experimental.pallas import tpu as pltpu
from jax.sharding import PartitionSpec as P

CAP = 8
NY = 4
NX = 4
STAGES = 4
WIDE = 896
NARROW = 256
MESH = pl.DeviceIdType.MESH
F32 = jnp.float32
BF16 = jnp.bfloat16


def dot(a, b):
    return jnp.dot(a, b, preferred_element_type=F32)


def loop(n, body):
    def step(i, carry):
        body(i)
        return carry

    lax.fori_loop(0, n, step, 0)


def span(start, size):
    return pl.ds(pl.multiple_of(start, 128), size)


def route(ids, gates):
    count = ids.shape[1]
    hits, chosen = [], []
    for expert in range(NY):
        match = ids == expert
        hits.append(jnp.sum(match.astype(F32), axis=0, keepdims=True))
        chosen.append(jnp.sum(jnp.where(match, gates, 0.0), axis=0, keepdims=True))
    tri = lax.broadcasted_iota(jnp.int32, (count, count), 0) <= lax.broadcasted_iota(jnp.int32, (count, count), 1)
    stacked = jnp.concatenate([jnp.broadcast_to(hit, (CAP, count)) for hit in hits], axis=0)
    slots = dot(stacked.astype(BF16), tri.astype(F32).astype(BF16)) - 1.0
    level = lax.rem(lax.broadcasted_iota(jnp.int32, (NY * CAP, count), 0), CAP).astype(F32)
    place = jnp.where(slots == level, stacked, 0.0)
    gate = jnp.concatenate([jnp.broadcast_to(row, (CAP, count)) for row in chosen], axis=0)
    return place, jnp.sum(place * gate, axis=1, keepdims=True)


def kernel(
    tok_hbm, cot_hbm, ids_hbm, gates_hbm, wg_hbm, wu_hbm, wd_hbm,
    fb, gg_hbm, gu_hbm, gd_hbm,
    tok, cot, ids, gates, place, gsl, wcat, wcatT, wd, wdT, sb, xs, x2d, s2d, part, own_send, own_recv,
    pair_send, pair_recv, hb, h16, dgu16, ob, rb, gg, gu, gd,
    in_sem, wsend, wrecv, zsend, recv, fsend, asend, arecv, bsend, brecv, hsend, hrecv,
    rsend, rrecv, osend, orecv, gsend, grecv, gown,
):
    quarter = wd.shape[1]
    p = lax.axis_index("pipe")
    e = lax.axis_index("expert")
    y = lax.div(e, 8)
    zh = lax.rem(lax.div(e, 4), 2)
    x = lax.rem(e, 4)
    yz = e - x
    h = lax.div(p, 4)
    q = p + h * (7 - 2 * p)
    shift = lax.rem(q, 2)
    u = lax.rem(x + 3 * shift, 4)
    role = lax.div(lax.rem(u + 1, 4), 2)
    other = 1 - role
    partner = lax.rem(u + 1 - 2 * lax.rem(u, 2) + shift, 4)
    twin = lax.rem(3 - u + shift, 4)
    across = lax.rem(x + 2, 4)
    inner = lax.div(lax.rem(lax.div(p, 2) + 1, 4), 2)
    gid = h * 2 + zh

    def rank_of(hh):
        return q + hh * (7 - 2 * q)

    def place_of(d):
        hh = lax.rem(h + lax.div(d, 2), 2)
        zz = lax.rem(zh + lax.rem(d, 2), 2)
        return hh, zz

    nearest = (0, 3 - inner, 2 + inner, 1)

    def remote(src, dst, ssem, rsem, rank, expert):
        return pltpu.make_async_remote_copy(
            src_ref=src, dst_ref=dst, send_sem=ssem, recv_sem=rsem,
            device_id=(rank, expert), device_id_type=MESH)

    def arrived(ref, sem):
        pltpu.make_async_copy(ref, ref, sem).wait()

    barrier = pltpu.get_barrier_semaphore()

    def greet(t):
        j, d, side = lax.div(t, 8), lax.rem(lax.div(t, 2), 4), lax.rem(t, 2)
        hh, zz = place_of(d)
        xx = x + side * (partner - x)
        pl.semaphore_signal(
            barrier, inc=1, device_id=(rank_of(hh), lax.rem(y + j, 4) * 8 + zz * 4 + xx), device_id_type=MESH)

    loop(31, lambda t: greet(t + 1))
    pl.semaphore_signal(barrier, inc=1, device_id=(p, yz + twin), device_id_type=MESH)

    mine, theirs = span(role * quarter, quarter), span(other * quarter, quarter)
    gate_cols, up_cols, down_rows = span(role * 256, 128), span(role * 256 + 128, 128), span(role * 128, 128)
    loads = [
        pltpu.make_async_copy(ids_hbm, ids, in_sem.at[0]),
        pltpu.make_async_copy(gates_hbm, gates, in_sem.at[1]),
        pltpu.make_async_copy(tok_hbm, tok, in_sem.at[2]),
        pltpu.make_async_copy(cot_hbm, cot, in_sem.at[3]),
        pltpu.make_async_copy(wg_hbm.at[mine, :], wcat.at[:, gate_cols], in_sem.at[4]),
        pltpu.make_async_copy(wu_hbm.at[mine, :], wcat.at[:, up_cols], in_sem.at[5]),
        pltpu.make_async_copy(wd_hbm.at[:, mine], wd.at[down_rows, :], in_sem.at[6]),
    ]
    weights = [
        remote(wg_hbm.at[theirs, :], wcat.at[:, gate_cols], wsend.at[0], wrecv.at[0], p, yz + partner),
        remote(wu_hbm.at[theirs, :], wcat.at[:, up_cols], wsend.at[1], wrecv.at[1], p, yz + partner),
        remote(wd_hbm.at[:, theirs], wd.at[down_rows, :], wsend.at[2], wrecv.at[2], p, yz + partner),
    ]
    for load in loads:
        load.start()
    for load in loads[:2]:
        load.wait()
    placed, gate_slot = route(ids[...], gates[...])
    place[...] = placed.astype(BF16)
    gsl[...] = gate_slot
    for load in loads[2:4]:
        load.wait()

    def slot_rows(ct):
        k, col = lax.div(ct, 2), lax.rem(ct, 2)
        hf, ro = lax.div(k, 2), lax.rem(k, 2)
        cols, to = span(ct * WIDE, WIDE), span(col * WIDE, WIDE)
        rows = dot(place[...], tok[:, cols])
        sb[:, hf, ro, 0, :, to] = rows.reshape(NY, CAP, WIDE).astype(BF16)
        raw = dot(place[...], cot[:, cols]) * gsl[...]
        sb[:, hf, ro, 1, :, to] = raw.reshape(NY, CAP, WIDE).astype(BF16)

    loop(8, slot_rows)
    pl.semaphore_wait(barrier, 32)

    own_s = y * 4 + gid
    local = pltpu.make_async_copy(sb.at[y, h, role], xs.at[x, own_s], recv.at[x, own_s])

    def zcopy(i, d, side):
        hh, zz = place_of(d)
        yy = lax.rem(y + 4 - i, 4)
        ro = role + side * (1 - 2 * role)
        xx = partner if side else x
        return remote(sb.at[yy, hh, ro], xs.at[x, own_s], zsend.at[i, d, side], recv.at[x, own_s],
                      rank_of(hh), yy * 8 + zz * 4 + xx)

    def send_far(i):
        for d in nearest[:0:-1]:
            zcopy(i, d, 1).start()
        zcopy(i, 0, 1).start()

    def send_out(i):
        send_near(i)
        send_far(i)

    def send_near(i):
        for d in nearest[:0:-1]:
            zcopy(i, d, 0).start()

        @pl.when(i == 0)
        def _():
            local.start()

        @pl.when(i > 0)
        def _():
            zcopy(i, 0, 0).start()

    def base(i):
        return lax.rem(y + i, 4) * 4

    def source(i, d):
        hh, zz = place_of(d)
        return base(i) + hh * 2 + zz

    def fcopy(s, side):
        c = partner if side else x
        return remote(xs.at[c, s], xs.at[c, s], fsend.at[side, s], recv.at[c, s], p, yz + twin)

    def forward(i):
        for d in nearest:
            s = source(i, d)
            for side, c in ((0, x), (1, partner)):
                arrived(xs.at[c, s], recv.at[c, s])
                fcopy(s, side).start()

    def rows_of(i):
        return span(i * 128, 128)

    def acopy(i):
        return remote(own_send.at[i], own_recv.at[i], asend.at[i], arecv.at[i], p, yz + partner)

    def bcopy(i):
        return remote(pair_send.at[i], pair_recv.at[i], bsend.at[i], brecv.at[i], 7 - p, e)

    def hcopy(i):
        return remote(hb.at[i, role], hb.at[i, role], hsend.at[i], hrecv.at[i], p, yz + partner)

    def first_dots(i):
        def rest(j):
            s = base(i) + j
            arrived(xs.at[twin, s], recv.at[twin, s])
            arrived(xs.at[across, s], recv.at[across, s])

        loop(4, rest)

        def flatten(c):
            to = pl.ds(pl.multiple_of(i * 128 + c * 32, 32), 32)
            x2d[to, :] = xs[c, pl.ds(base(i), 4), 0].astype(F32).reshape(32, quarter).astype(BF16)
            s2d[to, :] = xs[c, pl.ds(base(i), 4), 1].astype(F32).reshape(32, quarter).astype(BF16)

        loop(4, flatten)
        rows = rows_of(i)
        pre = dot(x2d[rows, :], wcat[...])
        dh = dot(s2d[rows, :], wdT[...])
        for k in range(2):
            part[i, k, :, 0:256] = pre[:, k * 256:k * 256 + 256]
            part[i, k, :, 256:384] = dh[:, k * 128:k * 128 + 128]
        own_send[i] = part[i, other].reshape(16, 8, 384).astype(BF16)
        acopy(i).start()

    def add_partner(i):
        arrived(own_recv.at[i], arecv.at[i])
        both = part[i, role] + own_recv[i].astype(F32).reshape(128, 384)
        part[i, role] = both
        pair_send[i] = both.reshape(16, 8, 384).astype(BF16)
        bcopy(i).start()

    def activate(i):
        arrived(pair_recv.at[i], brecv.at[i])
        whole = part[i, role] + pair_recv[i].astype(F32).reshape(128, 384)
        gate, up, dh = whole[:, 0:128], whole[:, 128:256], whole[:, 256:384]
        sigma = jax.nn.sigmoid(gate)
        active = gate * sigma
        hb[i, role, :, :, 0:128] = (active * up).reshape(16, 8, 128).astype(BF16)
        dgate = dh * up * sigma * (1.0 + gate * (1.0 - sigma))
        hb[i, role, :, :, 128:256] = dgate.reshape(16, 8, 128).astype(BF16)
        hb[i, role, :, :, 256:384] = (dh * active).reshape(16, 8, 128).astype(BF16)
        hcopy(i).start()

    def rcopy(s, side):
        c = across if side else twin
        return remote(ob.at[c, s], rb.at[side, s], rsend.at[side, s], rrecv.at[side, s], p, yz + twin)

    def second_dots(i):
        rows = rows_of(i)
        arrived(hb.at[i, other], hrecv.at[i])
        for k in range(2):
            flat = hb[i, k].astype(F32).reshape(128, 384).astype(BF16)
            h16[rows, k * 128:k * 128 + 128] = flat[:, 0:128]
            dgu16[rows, k * 256:k * 256 + 256] = flat[:, 128:384]

        def tile(ct):
            cols = span(ct * WIDE, WIDE)
            out = dot(h16[rows, :], wd[:, cols])
            ob[:, pl.ds(base(i), 4), 0, :, cols] = out.reshape(NX, 4, CAP, WIDE).astype(BF16)
            back = dot(dgu16[rows, :], wcatT[:, cols])
            ob[:, pl.ds(base(i), 4), 1, :, cols] = back.reshape(NX, 4, CAP, WIDE).astype(BF16)

        loop(2, tile)
        for d in nearest[::-1]:
            s = source(i, d)
            rcopy(s, 0).start()
            rcopy(s, 1).start()

    def seat(hf, ro, zz):
        return (hf * 2 + ro) * 2 + zz

    def ocopy(i, d, side):
        hh, zz = place_of(d)
        yy = lax.rem(y + i, 4)
        s = source(i, d)
        c = partner if side else x
        return remote(ob.at[c, s], fb.at[y, seat(h, role, zh)], osend.at[side, s], orecv.at[y, seat(h, role, zh)],
                      rank_of(hh), yy * 8 + zz * 4 + c)

    own_out = pltpu.make_async_copy(ob.at[x, own_s], fb.at[y, seat(h, role, zh)], orecv.at[y, seat(h, role, zh)])

    def add_twin(i, side):
        c = partner if side else x
        for d in nearest[::-1]:
            s = source(i, d)
            arrived(rb.at[side, s], rrecv.at[side, s])
            ob[c, s] = (ob[c, s].astype(F32) + rb[side, s].astype(F32)).astype(BF16)
            if side == 1 or d is not nearest[0]:
                ocopy(i, d, side).start()
                continue

            @pl.when(i == 0)
            def _():
                own_out.start()

            @pl.when(i > 0)
            def _():
                ocopy(i, d, side).start()

    def weight_grads(k):
        dguT = dgu16[:, span(k * 256, 256)].T
        hT = h16[:, span(k * 128, 128)].T

        def tile(ct):
            cols = span(ct * NARROW, NARROW)
            both = dot(dguT, x2d[:, cols]).T
            gg[k, cols, :] = both[:, 0:128].astype(BF16)
            gu[k, cols, :] = both[:, 128:256].astype(BF16)
            gd[k, :, cols] = dot(hT, s2d[:, cols]).astype(BF16)

        loop(quarter // NARROW, tile)

    grads_away = [
        remote(gg.at[other], gg_hbm.at[mine, :], gsend.at[0], grecv.at[0], p, yz + partner),
        remote(gu.at[other], gu_hbm.at[mine, :], gsend.at[1], grecv.at[1], p, yz + partner),
        remote(gd.at[other], gd_hbm.at[:, mine], gsend.at[2], grecv.at[2], p, yz + partner),
    ]
    grads_own = [
        pltpu.make_async_copy(gg.at[role], gg_hbm.at[mine, :], gown.at[0]),
        pltpu.make_async_copy(gu.at[role], gu_hbm.at[mine, :], gown.at[1]),
        pltpu.make_async_copy(gd.at[role], gd_hbm.at[:, mine], gown.at[2]),
    ]

    send_out(0)
    send_out(1)
    send_out(2)
    send_out(3)
    for copy in weights:
        copy.start()
    forward(0)
    for load in loads[4:]:
        load.wait()
    for copy in weights:
        copy.wait_recv()

    def turn_down(ct):
        cols = span(ct * NARROW, NARROW)
        wdT[cols, :] = wd[:, cols].T

    def turn_cat(ct):
        cols = span(ct * NARROW, NARROW)
        wcatT[:, cols] = wcat[cols, :].T

    loop(quarter // NARROW, turn_down)

    def turn_of(i):
        @pl.when(i < 4)
        def _():
            first_dots(i)

        @pl.when(jnp.logical_and(i >= 1, i < 5))
        def _():
            activate(i - 1)

        @pl.when(i == 0)
        def _():
            loop(quarter // NARROW, turn_cat)

        @pl.when(i < 3)
        def _():
            forward(i + 1)

        @pl.when(i < 4)
        def _():
            add_partner(i)

        @pl.when(jnp.logical_and(i >= 1, i < 5))
        def _():
            second_dots(i - 1)

        @pl.when(i >= 2)
        def _():
            add_twin(i - 2, 1)

        @pl.when(i >= 2)
        def _():
            add_twin(i - 2, 0)

        @pl.when(i == 4)
        def _():
            weight_grads(other)
            for copy in grads_away:
                copy.start()

    loop(6, turn_of)
    weight_grads(role)
    for copy in grads_own:
        copy.start()

    for copy in weights + grads_away:
        copy.wait_send()
    for i in range(STAGES):
        for side in range(2):
            for d in range(4):
                if (i, d, side) != (0, 0, 0):
                    zcopy(i, d, side).wait_send()

    def sent(i):
        for d in range(4):
            s = source(i, d)
            for side in range(2):
                fcopy(s, side).wait_send()
                rcopy(s, side).wait_send()
                if side == 1 or d > 0:
                    ocopy(i, d, side).wait_send()

        @pl.when(i > 0)
        def _():
            ocopy(i, 0, 0).wait_send()

        acopy(i).wait_send()
        bcopy(i).wait_send()
        hcopy(i).wait_send()

    loop(STAGES, sent)

    def landed(t):
        k, n = lax.div(t, 8), lax.rem(t, 8)
        arrived(fb.at[k, n], orecv.at[k, n])

    loop(32, landed)
    for copy in grads_own:
        copy.wait()
    for copy in grads_away:
        copy.wait_recv()


def finish(
    ids_ref, gates_ref, fb_hbm, gg_in, gu_in, gd_in, mixed_hbm, igrad_hbm, gg_out, gu_out, gd_out,
    fb, mixed, igrad, gg, gu, gd, in_sem, out_sem, pass_sem,
):
    quarter = fb.shape[-1]
    grads = ((gg_in, gg, gg_out), (gu_in, gu, gu_out), (gd_in, gd, gd_out))
    enter = [pltpu.make_async_copy(grad[0], grad[1], pass_sem.at[0, n]) for n, grad in enumerate(grads)]
    leave = [pltpu.make_async_copy(grad[1], grad[2], pass_sem.at[1, n]) for n, grad in enumerate(grads)]
    fetch = [
        pltpu.make_async_copy(fb_hbm.at[:, pl.ds(2 * n, 2)], fb.at[:, pl.ds(2 * n, 2)], in_sem.at[n]) for n in range(4)
    ]
    for copy in fetch + enter:
        copy.start()
    place, gsl = route(ids_ref[...], gates_ref[...])
    placeT = place.T.astype(BF16)
    stores = []
    for n in range(4):
        fetch[n].wait()
        for col in range(0, quarter, WIDE):
            fr, to = pl.ds(col, WIDE), pl.ds(n * quarter + col, WIDE)

            def both(k):
                return (fb[:, 2 * n, k, :, fr].astype(F32) + fb[:, 2 * n + 1, k, :, fr].astype(F32)).reshape(32, WIDE)

            mixed[:, to] = dot(placeT, (both(0) * gsl).astype(BF16)).astype(BF16)
            igrad[:, to] = dot(placeT, both(1).astype(BF16)).astype(BF16)
        if n == 0:
            for get, put in zip(enter, leave):
                get.wait()
                put.start()
        cols = pl.ds(n * quarter, quarter)
        stores += [
            pltpu.make_async_copy(mixed.at[:, cols], mixed_hbm.at[:, cols], out_sem.at[n, 0]),
            pltpu.make_async_copy(igrad.at[:, cols], igrad_hbm.at[:, cols], out_sem.at[n, 1]),
        ]
        stores[-2].start()
        stores[-1].start()
    for copy in stores + leave:
        copy.wait()


def per_device(tokens, cotangent, expert_ids, gate_weights, w_gate, w_up, w_down):
    tok_count, width = tokens.shape
    half, quarter = width // 2, width // 4
    ids, gates = expert_ids.T, gate_weights.T
    dma = pltpu.SemaphoreType.DMA
    vmem = pltpu.VMEM
    piece = (2, CAP, quarter)
    swap = (STAGES, 16, 8, 384)
    any_spec = pl.BlockSpec(memory_space=pl.ANY)
    outs = pl.pallas_call(
        kernel,
        out_shape=(
            jax.ShapeDtypeStruct((NY, 8) + piece, BF16),
            jax.ShapeDtypeStruct((half, 128), BF16),
            jax.ShapeDtypeStruct((half, 128), BF16),
            jax.ShapeDtypeStruct((128, half), BF16),
        ),
        in_specs=[any_spec] * 7,
        out_specs=[any_spec] * 4,
        scratch_shapes=[
            vmem((tok_count, width), BF16),
            vmem((tok_count, width), BF16),
            vmem(ids.shape, jnp.int32),
            vmem(gates.shape, F32),
            vmem((32, tok_count), BF16),
            vmem((32, 1), F32),
            vmem((quarter, 512), BF16),
            vmem((512, quarter), BF16),
            vmem((256, quarter), BF16),
            vmem((quarter, 256), BF16),
            vmem((NY, 2, 2) + piece, BF16),
            vmem((NX, 16) + piece, BF16),
            vmem((512, quarter), BF16),
            vmem((512, quarter), BF16),
            vmem((STAGES, 2, 128, 384), F32),
            vmem(swap, BF16),
            vmem(swap, BF16),
            vmem(swap, BF16),
            vmem(swap, BF16),
            vmem((STAGES, 2, 16, 8, 384), BF16),
            vmem((512, 256), BF16),
            vmem((512, 512), BF16),
            vmem((NX, 16) + piece, BF16),
            vmem((2, 16) + piece, BF16),
            vmem((2, quarter, 128), BF16),
            vmem((2, quarter, 128), BF16),
            vmem((2, 128, quarter), BF16),
            dma((7,)),
            dma((3,)),
            dma((3,)),
            dma((STAGES, 4, 2)),
            dma((NX, 16)),
            dma((2, 16)),
            dma((STAGES,)),
            dma((STAGES,)),
            dma((STAGES,)),
            dma((STAGES,)),
            dma((STAGES,)),
            dma((STAGES,)),
            dma((2, 16)),
            dma((2, 16)),
            dma((2, 16)),
            dma((NY, 8)),
            dma((3,)),
            dma((3,)),
            dma((3,)),
        ],
        compiler_params=pltpu.CompilerParams(
            collective_id=0, has_side_effects=True, vmem_limit_bytes=56 * 1024 * 1024
        ),
    )(tokens, cotangent, ids, gates, w_gate[0], w_up[0], w_down[0])
    whole = pl.BlockSpec(memory_space=vmem)
    mixed, igrad, gg, gu, gd = pl.pallas_call(
        finish,
        out_shape=(
            jax.ShapeDtypeStruct((tok_count, width), BF16),
            jax.ShapeDtypeStruct((tok_count, width), BF16),
            jax.ShapeDtypeStruct((half, 128), BF16),
            jax.ShapeDtypeStruct((half, 128), BF16),
            jax.ShapeDtypeStruct((128, half), BF16),
        ),
        in_specs=[whole] * 2 + [any_spec] * 4,
        out_specs=[any_spec] * 5,
        scratch_shapes=[
            vmem((NY, 8) + piece, BF16),
            vmem((tok_count, width), BF16),
            vmem((tok_count, width), BF16),
            vmem((half, 128), BF16),
            vmem((half, 128), BF16),
            vmem((128, half), BF16),
            dma((4,)),
            dma((4, 2)),
            dma((2, 3)),
        ],
        compiler_params=pltpu.CompilerParams(vmem_limit_bytes=56 * 1024 * 1024),
    )(ids, gates, *outs)
    return mixed, igrad, gg[None], gu[None], gd[None]


def solution(mesh):
    return jax.shard_map(
        per_device,
        mesh=mesh,
        in_specs=(
            P(("pipe", "expert"), None),
            P(("pipe", "expert"), None),
            P(("pipe", "expert"), None),
            P(("pipe", "expert"), None),
            P("pipe", None, "expert"),
            P("pipe", None, "expert"),
            P("pipe", "expert", None),
        ),
        out_specs=(
            P(("pipe", "expert"), None),
            P(("pipe", "expert"), None),
            P("pipe", None, "expert"),
            P("pipe", None, "expert"),
            P("pipe", "expert", None),
        ),
        check_vma=False,
    )
```
